128 devices in a mesh: shard: 16 (over x, z), blk: 8 (over y, core).
Axes of the slice: x: 4, y: 4, z: 4, core: 2. Of those that a mesh axis runs over, the one named last changes fastest.
Arguments:
- codes: int32 [131072, 128], P(('shard', 'blk')), may hold values from 0 to 255
- cluster_ids: int32 [131072], P(('shard', 'blk')), may hold values from 0 to 1023, as said below
- cluster_owner: int32 [1024], replicated, may hold values from 0 to 15, as said below
- left_pair: int32 [1024], replicated, may hold values from 0 to 7
- codebook: bfloat16 [128, 256, 8], replicated, may hold values from -6 to 6
Outputs:
- within_max: float32 [131072], P(('shard', 'blk'))
- neighbour_max: float32 [131072], P(('shard', 'blk'))
The draws below stay inside these ranges and needn't reach their ends.
Inputs may be any that keep to these rules, and one draw needn't show every extreme that they name: `cluster_ids`: row r (of device block (r // 1024)) belongs to a cluster of column (r // 1024) % 8, that is an id from column * 128 up to (column + 1) * 128 - 1. In each aligned block of 1024 rows at most 128 rows belong to clusters of any one owner; in every column one owner receives exactly 128 rows from each of the column's 16 blocks. `cluster_owner`: within each column of 128 consecutive clusters every owner owns exactly 8 clusters.
All inputs are finite; a program needn't handle non-finite values.
Results may differ from the reference program's by a relative error of at most 0.0015.
Values may be sent and summed in bfloat16 or wider, within the bound.
No kernel may reach another device: no remote copies, remote signals or barrier semaphores. Data moves between devices by JAX's collectives and lax.ppermute only.
A program may use at most 64 MiB of HBM per device.

```python
import math
import jax
import jax.numpy as jnp
import numpy as np
from jax import lax

EMB = 1024
SUBQ = 128
CODES_K = 256
SUB = 8
ROWS_DEV = 1024
CPD = 8
RECV = 2048
ROWS = 131072
CLUSTERS = 1024
N_SHARD = 16
N_BLK = 8


def column_layout(key):
    span = CPD * N_SHARD
    split_keys = jax.random.split(key, N_BLK)
    orders = jax.vmap(lambda one_key: jax.random.permutation(one_key, span))(split_keys)
    return (orders // CPD).astype(jnp.int32)


def draw_cluster_owner(key, part):
    owners = column_layout(key)
    return owners.reshape(N_BLK * CPD * N_SHARD).astype(jnp.int32)


def draw_cluster_ids(key, part):
    owners = column_layout(key)
    key = jax.random.fold_in(key, 11)
    span = CPD * N_SHARD
    capacity = 2 * ROWS_DEV // N_SHARD
    half_cap = capacity // 2
    devices_all = N_SHARD * N_BLK
    places = jnp.arange(span, dtype=jnp.int32)
    by_owner = jnp.argsort(owners * span + places[None, :], axis=1).astype(jnp.int32)
    full_owner = jax.random.randint(jax.random.fold_in(key, 1), (N_BLK,), 0, N_SHARD).astype(jnp.int32)
    device_ids = jnp.arange(devices_all, dtype=jnp.int32)
    cycle_of = device_ids % N_BLK
    device_full = full_owner[cycle_of]
    other_keys = jax.random.split(jax.random.fold_in(key, 2), devices_all)
    others = jax.vmap(lambda one_key: jax.random.permutation(one_key, N_SHARD - 1))(other_keys).astype(jnp.int32)
    others = others + (others >= device_full[:, None]).astype(jnp.int32)
    swings = jax.random.randint(jax.random.fold_in(key, 3), (devices_all, (N_SHARD - 2) // 2), 0, half_cap + 1).astype(jnp.int32)
    paired = jnp.stack([half_cap + swings, half_cap - swings], axis=2).reshape(devices_all, N_SHARD - 2)
    amounts = jnp.concatenate([jnp.zeros((devices_all, 1), jnp.int32), paired], axis=1)
    owner_ids = jnp.arange(N_SHARD, dtype=jnp.int32)
    counts = jnp.sum(jnp.where(others[:, :, None] == owner_ids[None, None, :], amounts[:, :, None], 0), axis=1)
    counts = counts + jnp.where(device_full[:, None] == owner_ids[None, :], capacity, 0)
    ends = jnp.cumsum(counts, axis=1).astype(jnp.int32)
    row_ids = jnp.arange(ROWS_DEV, dtype=jnp.int32)
    row_owner = jnp.sum((row_ids[None, :, None] >= ends[:, None, :]).astype(jnp.int32), axis=2)
    shuffle_keys = jax.random.split(jax.random.fold_in(key, 4), devices_all)
    shuffles = jax.vmap(lambda one_key: jax.random.permutation(one_key, ROWS_DEV))(shuffle_keys).astype(jnp.int32)
    row_owner = jnp.take_along_axis(row_owner, shuffles, axis=1)
    slots = jax.random.randint(jax.random.fold_in(key, 5), (devices_all, ROWS_DEV), 0, CPD).astype(jnp.int32)
    picks = jnp.take_along_axis(by_owner[cycle_of], row_owner * CPD + slots, axis=1)
    cluster_list = cycle_of[:, None] * span + picks
    return cluster_list.reshape(devices_all * ROWS_DEV).astype(jnp.int32)


def set_ends(values, rng, smallest, largest):
    extent = values.shape
    place = [jax.random.randint(jax.random.fold_in(rng, axis), (), 0, extent[axis]) for axis in range(len(extent))]
    values = values.at[tuple(place)].set(smallest)
    longest = extent.index(max(extent))
    place[longest] = (place[longest] + 1) % extent[longest]
    return values.at[tuple(place)].set(largest)


def rank_table(count, lean):
    portions = [(1 << 20) // math.isqrt(rank ** lean) + 1 for rank in range(1, count + 1)]
    spread = 1 + sum(portions) // (1 << 30)
    return np.cumsum(np.array([max(1, weight // spread) for weight in portions]))


def ranked(rng, shape, number_of, slope):
    table = rank_table(number_of, slope)
    lot = jax.random.randint(jax.random.fold_in(rng, 1), shape, 0, int(table[number_of - 1]))
    grade = jnp.searchsorted(jnp.asarray(table, jnp.int32), lot, side="right")
    return jax.random.permutation(jax.random.fold_in(rng, 2), number_of)[grade].astype(jnp.int32)


def noise(key, shape, width, most, kind=jnp.bfloat16):
    array = width * jax.random.normal(key, shape, jnp.float32)
    return jnp.clip(array, min=-most, max=most).astype(kind)


def setup_inputs(seed: int = 0) -> dict:
    key_of = jax.random.split(jax.random.key(seed), 6)
    return {
        "codes": set_ends(ranked(key_of[0], (ROWS, SUBQ), CODES_K, 3), jax.random.fold_in(key_of[0], 3), 0, CODES_K - 1).astype(jnp.int32),
        "cluster_ids": draw_cluster_ids(jax.random.fold_in(key_of[5], 71), 0),
        "cluster_owner": draw_cluster_owner(jax.random.fold_in(key_of[5], 71), 0),
        "left_pair": set_ends(jax.random.randint(key_of[3], (CLUSTERS,), 0, CPD), jax.random.fold_in(key_of[3], 1), 0, CPD - 1).astype(jnp.int32),
        "codebook": noise(key_of[4], (SUBQ, CODES_K, SUB), 1.0, 6.0),
    }


norm_epsilon = 1e-06

def group_rows(order_padded, starts, counts, group_id):
    members = lax.dynamic_slice_in_dim(order_padded, starts[group_id], RECV)
    live = jnp.arange(RECV, dtype=jnp.int32) < counts[group_id]
    return (members, live)

def place_values(values, members, live, total_rows):
    target = jnp.where(live, members, total_rows).reshape(-1)
    empty = jnp.full((total_rows,), -1.0, jnp.float32)
    return empty.at[target].set(values.reshape(-1), mode='drop')

def reference(codes, cluster_ids, cluster_owner, left_pair, codebook):
    total_rows = codes.shape[0]
    code_table = codebook.reshape(SUBQ * CODES_K, SUB)
    flat_codes = codes + (jnp.arange(SUBQ, dtype=jnp.int32) * CODES_K)[None, :]
    decoded = jnp.take(code_table, flat_codes, axis=0).reshape(total_rows, EMB).astype(jnp.float32)
    unit_rows = (decoded * lax.rsqrt(lax.optimization_barrier(jnp.sum(decoded * decoded, axis=1, keepdims=True)) + norm_epsilon)).astype(jnp.bfloat16)
    span = CPD * N_SHARD
    owners = cluster_owner.reshape(N_BLK, span)
    places = jnp.arange(span, dtype=jnp.int32)
    same_owner = owners[:, :, None] == owners[:, None, :]
    earlier = places[None, :] < places[:, None]
    slot_table = lax.optimization_barrier(jnp.sum(same_owner & earlier[None, :, :], axis=2)).reshape(-1).astype(jnp.int32)
    row_slot = slot_table[cluster_ids]
    row_owner = cluster_owner[cluster_ids]
    column = cluster_ids // span
    group = (column * N_SHARD + row_owner).astype(jnp.int32)
    group_total = N_BLK * N_SHARD
    order = jnp.argsort(group, stable=True).astype(jnp.int32)
    counts = jnp.zeros((group_total,), jnp.int32).at[group].add(1)
    starts = (jnp.cumsum(counts) - counts).astype(jnp.int32)
    order_padded = jnp.concatenate([order, jnp.zeros((RECV,), jnp.int32)])
    partner_row = left_pair[cluster_ids]
    positions = jnp.arange(RECV, dtype=jnp.int32)
    not_self = positions[:, None] != positions[None, :]

    def one_group(group_id):
        members, live = group_rows(order_padded, starts, counts, group_id)
        embeds = unit_rows[members]
        slots = jnp.where(live, row_slot[members], -1)
        partner_keys = jnp.where(live, partner_row[members], -2)
        left_group = (group_id // N_SHARD + N_BLK - 1) % N_BLK * N_SHARD + group_id % N_SHARD
        left_members, left_live = group_rows(order_padded, starts, counts, left_group)
        left_embeds = unit_rows[left_members]
        left_slots = jnp.where(left_live, row_slot[left_members], -1)
        within = jnp.dot(embeds, embeds.T, preferred_element_type=jnp.float32)
        within_mask = (slots[:, None] == slots[None, :]) & (slots[None, :] >= 0) & not_self
        within_best = lax.optimization_barrier(jnp.max(jnp.where(within_mask, within, -1.0), axis=1))
        across = jnp.dot(embeds, left_embeds.T, preferred_element_type=jnp.float32)
        link_mask = (partner_keys[:, None] == left_slots[None, :]) & (left_slots[None, :] >= 0)
        masked = jnp.where(link_mask, across, -1.0)
        return (within_best, lax.optimization_barrier(jnp.max(masked, axis=1)), lax.optimization_barrier(jnp.max(masked, axis=0)), members, live, left_members, left_live)
    within_best, from_left, for_left, members, live, left_members, left_live = lax.map(one_group, jnp.arange(group_total, dtype=jnp.int32))
    within_max = place_values(within_best, members, live, total_rows)
    left_values = place_values(from_left, members, live, total_rows)
    right_values = place_values(for_left, left_members, left_live, total_rows)
    return (within_max, jnp.maximum(left_values, right_values))
```

```python
import functools

import jax
import jax.numpy as jnp
from jax import lax
from jax.experimental import pallas as pl
from jax.experimental.pallas import tpu as pltpu
from jax.sharding import PartitionSpec as P

EMB = 1024
SUBQ = 128
SUB = 8
CODES_K = 256
CPD = 8
LANES = 128
SHARDS = 16
CAP = 128
RECV = SHARDS * CAP
BLOCK = SUBQ + 16
norm_epsilon = 1e-06

VMEM = pl.BlockSpec(memory_space=pltpu.VMEM)
PARAMS = pltpu.CompilerParams(vmem_limit_bytes=48 << 20)


def lane_gather(table, index):
    numbers = lax.GatherDimensionNumbers(
        offset_dims=(),
        collapsed_slice_dims=(1,),
        start_index_map=(1,),
        operand_batching_dims=(0,),
        start_indices_batching_dims=(0,),
    )
    return lax.gather(
        table,
        index[..., None],
        numbers,
        slice_sizes=(1, 1),
        mode=lax.GatherScatterMode.PROMISE_IN_BOUNDS,
    )


def iota(shape, axis):
    return lax.broadcasted_iota(jnp.int32, shape, axis)


def route_kernel(codes_ref, ids_ref, owner_ref, pair_ref, send_ref, dest_ref, rank_ref):
    column = lax.axis_index("blk")
    owner_row = owner_ref[pl.ds(column, 1), :]
    pair_row = pair_ref[pl.ds(column, 1), :]
    owner_sq = jnp.broadcast_to(owner_row, (LANES, LANES))
    sub, lane = iota((LANES, LANES), 0), iota((LANES, LANES), 1)
    same = (owner_sq.T == owner_sq) & (sub < lane)
    slot_row = jnp.sum(same.astype(jnp.int32), axis=0, keepdims=True)
    local = ids_ref[...] - column * LANES
    full = (8, LANES)
    dest = lane_gather(jnp.broadcast_to(owner_row, full), local)
    slot = lane_gather(jnp.broadcast_to(slot_row, full), local)
    pair = lane_gather(jnp.broadcast_to(pair_row, full), local)
    member = jnp.concatenate([(dest == o).astype(jnp.float32) for o in range(SHARDS)], axis=0)
    member = member.astype(jnp.bfloat16)
    before = (sub < lane).astype(jnp.bfloat16)
    in_row = jnp.dot(member, before, preferred_element_type=jnp.float32)
    above = ((sub // 8 == lane // 8) & (lane < sub)).astype(jnp.bfloat16)
    rows_above = jnp.dot(above, member, preferred_element_type=jnp.float32).astype(jnp.bfloat16)
    ones = jnp.ones((LANES, LANES), jnp.bfloat16)
    count = in_row + jnp.dot(rows_above, ones, preferred_element_type=jnp.float32)
    rank = jnp.zeros(full, jnp.float32)
    for o in range(SHARDS):
        rank = jnp.where(dest == o, count[o * 8 : (o + 1) * 8, :], rank)
    rank = rank.astype(jnp.int32)
    dest_ref[...] = dest
    rank_ref[...] = rank
    codes_t = codes_ref[...].astype(jnp.float32).T
    slot_f = (slot + 1).astype(jnp.float32)
    pair_f = (pair + 1).astype(jnp.float32)
    slot_line = jnp.concatenate([slot_f[k : k + 1, :] for k in range(8)], axis=1)
    pair_line = jnp.concatenate([pair_f[k : k + 1, :] for k in range(8)], axis=1)
    tail_row = iota((16, 1024), 0)
    tail = jnp.where(tail_row == 0, slot_line, jnp.where(tail_row == 1, pair_line, 0.0))
    left = jnp.concatenate([codes_t, tail], axis=0).astype(jnp.bfloat16)
    for o in range(SHARDS):
        key = jnp.where(dest == o, rank, -1)
        pick = jnp.concatenate(
            [
                (jnp.broadcast_to(key[k : k + 1, :], (LANES, LANES)) == sub).astype(jnp.float32)
                for k in range(8)
            ],
            axis=1,
        ).astype(jnp.bfloat16)
        block = lax.dot_general(
            left, pick, (((1,), (1,)), ((), ())), preferred_element_type=jnp.float32
        )
        send_ref[o] = block.astype(jnp.bfloat16)


def decode(got_ref, table_ref, norm_ref, scale_ref, ut_ref):
    def add_norms(g, totals):
        totals = list(totals)
        part = pl.ds(pl.multiple_of(g * 16, 16), 16)
        low, high = norm_ref[part, :LANES], norm_ref[part, LANES:]
        for j in range(SHARDS):
            code = got_ref[j, part, :].astype(jnp.int32)
            rest = code & 127
            totals[j] = totals[j] + jnp.where(
                code < LANES, lane_gather(low, rest), lane_gather(high, rest)
            )
        return tuple(totals)

    zero = jnp.zeros((16, LANES), jnp.float32)
    totals = lax.fori_loop(0, SUBQ // 16, add_norms, (zero,) * SHARDS)
    for j in range(SHARDS):
        norm = jnp.sum(totals[j], axis=0, keepdims=True)
        scale_ref[j] = jnp.broadcast_to(lax.rsqrt(norm + norm_epsilon), (16, LANES))

    def one_group(g, carry):
        part = pl.ds(pl.multiple_of(g * 16, 16), 16)
        tables = [(table_ref[g, i, :, :LANES], table_ref[g, i, :, LANES:]) for i in range(SUB)]
        for j in range(SHARDS):
            code = got_ref[j, part, :].astype(jnp.int32).astype(jnp.int16)
            rest = code & 127
            is_low = code < LANES
            scale = scale_ref[j]
            for i in range(SUB):
                value = jnp.where(
                    is_low, lane_gather(tables[i][0], rest), lane_gather(tables[i][1], rest)
                )
                rows = pl.ds(pl.multiple_of(g * 128 + i * 16, 16), 16)
                ut_ref[rows, j * LANES : (j + 1) * LANES] = (
                    value.astype(jnp.float32) * scale
                ).astype(jnp.bfloat16)
        return carry

    lax.fori_loop(0, SUBQ // 16, one_group, 0, unroll=2)


def own_kernel(got_ref, table_ref, norm_ref, ut_ref, u_ref, scale_ref):
    decode(got_ref, table_ref, norm_ref, scale_ref, ut_ref)
    side = 256
    eye = (iota((side, side), 0) == iota((side, side), 1)).astype(jnp.bfloat16)

    def turn(i, carry):
        rows = pl.ds(pl.multiple_of(i * side, side), side)
        for f in range(EMB // side):
            u_ref[rows, f * side : (f + 1) * side] = lax.dot_general(
                eye,
                ut_ref[f * side : (f + 1) * side, rows],
                (((1,), (1,)), ((), ())),
                preferred_element_type=jnp.float32,
            ).astype(jnp.bfloat16)
        return carry

    lax.fori_loop(0, RECV // side, turn, 0)


def spread_keys(got_ref, line, keys_ref):
    for j in range(SHARDS):
        key = got_ref[j, SUBQ : SUBQ + 16, :].astype(jnp.float32)[line : line + 1, :]
        keys_ref[j * LANES : (j + 1) * LANES, :] = jnp.broadcast_to(key, (LANES, LANES)).T


def key_lines(got_ref, line, empty):
    keys = [
        got_ref[j, SUBQ : SUBQ + 16, :].astype(jnp.float32)[line : line + 1, :]
        for j in range(SHARDS)
    ]
    return [jnp.where(key == 0.0, empty, key) for key in keys]


SIDE = 256


def fold_lanes(row_best):
    return jnp.max(row_best.T, axis=0, keepdims=True)


def across_kernel(got_ref, left_ref, table_ref, norm_ref, u_ref, out_ref, ut_ref, scale_ref, keys_ref, line_ref, best_ref):
    decode(left_ref, table_ref, norm_ref, scale_ref, ut_ref)
    spread_keys(got_ref, 1, keys_ref)
    lines = key_lines(left_ref, 0, -1.0)
    for j in range(SHARDS):
        line_ref[j] = jnp.broadcast_to(lines[j], (8, LANES))
    best_ref[...] = jnp.full(best_ref.shape, -1.0, jnp.float32)

    def one_tile(i, carry):
        rows = pl.ds(pl.multiple_of(i * SIDE, SIDE), SIDE)
        key = keys_ref[rows, :].reshape(SIDE // 8, 8, LANES)
        u = u_ref[rows, :]
        row_best = jnp.full((SIDE // 8, 8, LANES), -1.0, jnp.float32)
        for n in range(RECV // SIDE):
            scores = jnp.dot(
                u, ut_ref[:, n * SIDE : (n + 1) * SIDE], preferred_element_type=jnp.float32
            )
            for h in range(SIDE // LANES):
                j = n * (SIDE // LANES) + h
                part = scores[:, h * LANES : (h + 1) * LANES].reshape(SIDE // 8, 8, LANES)
                part = jnp.where(key == line_ref[j][None], part, -1.0)
                row_best = jnp.maximum(row_best, part)
                best_ref[j] = jnp.maximum(best_ref[j], jnp.max(part, axis=0))
        line = fold_lanes(row_best.reshape(SIDE, LANES))
        for h in range(SIDE // LANES):
            out_ref[0, pl.ds(i * (SIDE // LANES) + h, 1), :] = line[:, h * LANES : (h + 1) * LANES]
        return carry

    lax.fori_loop(0, RECV // SIDE, one_tile, 0)
    for j in range(SHARDS):
        out_ref[1, j : j + 1, :] = jnp.max(best_ref[j], axis=0, keepdims=True)


def within_kernel(got_ref, u_ref, ut_ref, out_ref, keys_ref, line_ref, best_ref):
    spread_keys(got_ref, 0, keys_ref)
    lines = key_lines(got_ref, 0, -1.0)
    for j in range(SHARDS):
        line_ref[j] = jnp.broadcast_to(lines[j], (8, LANES))
    best_ref[...] = jnp.full(best_ref.shape, -1.0, jnp.float32)
    sub = iota((SIDE // 8, 8, LANES), 0) * 8 + iota((SIDE // 8, 8, LANES), 1)
    lane = iota((SIDE // 8, 8, LANES), 2)

    def one_tile(i, carry):
        rows = pl.ds(pl.multiple_of(i * SIDE, SIDE), SIDE)
        key = keys_ref[rows, :].reshape(SIDE // 8, 8, LANES)
        u = u_ref[rows, :]

        def one_part(n, row_best):
            scores = jnp.dot(
                u,
                ut_ref[:, pl.ds(pl.multiple_of(n * SIDE, SIDE), SIDE)],
                preferred_element_type=jnp.float32,
            )
            for h in range(SIDE // LANES):
                j = n * (SIDE // LANES) + h
                part = scores[:, h * LANES : (h + 1) * LANES].reshape(SIDE // 8, 8, LANES)
                ok = (key == line_ref[j][None]) & (sub + i * SIDE != lane + j * LANES)
                part = jnp.where(ok, part, -1.0)
                row_best = jnp.maximum(row_best, part)
                best_ref[j] = jnp.maximum(best_ref[j], jnp.max(part, axis=0))
            return row_best

        row_best = jnp.full((SIDE // 8, 8, LANES), -1.0, jnp.float32)
        row_best = lax.fori_loop(i, RECV // SIDE, one_part, row_best)
        line = fold_lanes(row_best.reshape(SIDE, LANES))
        for h in range(SIDE // LANES):
            out_ref[pl.ds(i * (SIDE // LANES) + h, 1), :] = line[:, h * LANES : (h + 1) * LANES]
        return carry

    lax.fori_loop(0, RECV // SIDE, one_tile, 0)
    for j in range(SHARDS):
        out_ref[j : j + 1, :] = jnp.maximum(
            out_ref[j : j + 1, :], jnp.max(best_ref[j], axis=0, keepdims=True)
        )


def pick_kernel(got_ref, dest_ref, rank_ref, within_ref, near_ref):
    dest, rank = dest_ref[...], rank_ref[...]
    within = jnp.zeros((8, LANES), jnp.float32)
    near = within
    for o in range(SHARDS):
        here = dest == o
        first = jnp.broadcast_to(got_ref[o, 0:1, :], (8, LANES))
        second = jnp.broadcast_to(got_ref[o, 1:2, :], (8, LANES))
        within = jnp.where(here, lane_gather(first, rank), within)
        near = jnp.where(here, lane_gather(second, rank), near)
    within_ref[...] = within
    near_ref[...] = near


def kernel_call(body, shapes, count, scratch=(), name=None, flops=0):
    return pl.pallas_call(
        body,
        out_shape=shapes,
        in_specs=[VMEM] * count,
        out_specs=[VMEM] * len(shapes),
        scratch_shapes=list(scratch),
        compiler_params=PARAMS,
        name=name,
        cost_estimate=pl.CostEstimate(flops=flops, bytes_accessed=1 << 20, transcendentals=0),
    )


def shape(dims, kind):
    return jax.ShapeDtypeStruct(dims, kind)


bf16, f32, i32 = jnp.bfloat16, jnp.float32, jnp.int32
K_ROUTE = (route_kernel, [shape((SHARDS, BLOCK, LANES), bf16), shape((8, LANES), i32), shape((8, LANES), i32)], 4)
K_OWN = (own_kernel, [shape((EMB, RECV), bf16), shape((RECV, EMB), bf16)], 3, [pltpu.VMEM((SHARDS, 16, LANES), f32)])
K_ACROSS = (
    across_kernel,
    [shape((2, SHARDS, LANES), f32)],
    5,
    [
        pltpu.VMEM((EMB, RECV), bf16),
        pltpu.VMEM((SHARDS, 16, LANES), f32),
        pltpu.VMEM((RECV, LANES), f32),
        pltpu.VMEM((SHARDS, 8, LANES), f32),
        pltpu.VMEM((SHARDS, 8, LANES), f32),
    ],
)
K_WITHIN = (
    within_kernel,
    [shape((SHARDS, LANES), f32)],
    3,
    [
        pltpu.VMEM((RECV, LANES), f32),
        pltpu.VMEM((SHARDS, 8, LANES), f32),
        pltpu.VMEM((SHARDS, 8, LANES), f32),
    ],
)
K_PICK = (pick_kernel, [shape((8, LANES), f32), shape((8, LANES), f32)], 3)


def from_behind(x, axis, by):
    peers = lax.axis_size(axis)
    return lax.ppermute(x, axis, [(i, (i + by) % peers) for i in range(peers)])


def tables_of(codebook):
    turned = jnp.swapaxes(codebook, 1, 2)
    squares = turned.astype(f32)
    norms = jnp.sum(squares * squares, axis=1)
    table = turned.reshape(SUBQ // 16, 16, SUB, CODES_K).transpose(0, 2, 1, 3)
    return table, norms


def on_device(codes, cluster_ids, cluster_owner, left_pair, codebook):
    send, dest, rank = kernel_call(*K_ROUTE, name="route", flops=1 << 30)(
        codes,
        cluster_ids.reshape(8, LANES),
        cluster_owner.reshape(8, LANES),
        left_pair.reshape(8, LANES),
    )
    table, norms = tables_of(codebook)
    got = lax.all_to_all(send, "shard", split_axis=0, concat_axis=0, tiled=True)
    left = from_behind(got, "blk", 1)
    ut, u = kernel_call(*K_OWN, name="own", flops=8 << 30)(got, table, norms)
    (crossed,) = kernel_call(*K_ACROSS, name="across", flops=16 << 30)(got, left, table, norms, u)
    from_right = from_behind(crossed[1], "blk", -1)
    (within,) = kernel_call(*K_WITHIN, name="within", flops=8 << 30)(got, u, ut)
    near = jnp.maximum(crossed[0], from_right)
    answers = jnp.stack([within, near], axis=1)
    back = lax.all_to_all(answers, "shard", split_axis=0, concat_axis=0, tiled=True)
    within_max, near_max = kernel_call(*K_PICK, name="pick")(back, dest, rank)
    return within_max.reshape(-1), near_max.reshape(-1)


def solution(mesh):
    in_specs = (P(("shard", "blk"), None), P(("shard", "blk")), P(), P(), P())
    out_specs = (P(("shard", "blk")), P(("shard", "blk")))
    return jax.shard_map(
        on_device, mesh=mesh, in_specs=in_specs, out_specs=out_specs, check_vma=False
    )
```

```python
import functools

import jax
import jax.numpy as jnp
from jax import lax
from jax.experimental import pallas as pl
from jax.experimental.pallas import tpu as pltpu
from jax.sharding import PartitionSpec as P

EMB = 1024
SUBQ = 128
SUB = 8
CODES_K = 256
CPD = 8
LANES = 128
SHARDS = 16
CAP = 128
RECV = SHARDS * CAP
BLOCK = SUBQ + 16
norm_epsilon = 1e-06

VMEM = pl.BlockSpec(memory_space=pltpu.VMEM)


def lane_gather(table, index):
    numbers = lax.GatherDimensionNumbers(
        offset_dims=(),
        collapsed_slice_dims=(1,),
        start_index_map=(1,),
        operand_batching_dims=(0,),
        start_indices_batching_dims=(0,),
    )
    return lax.gather(
        table,
        index[..., None],
        numbers,
        slice_sizes=(1, 1),
        mode=lax.GatherScatterMode.PROMISE_IN_BOUNDS,
    )


def iota(shape, axis):
    return lax.broadcasted_iota(jnp.int32, shape, axis)


def route_kernel(codes_ref, ids_ref, owner_ref, pair_ref, send_ref, dest_ref, rank_ref):
    column = lax.axis_index("blk")
    owner_row = owner_ref[pl.ds(column, 1), :]
    pair_row = pair_ref[pl.ds(column, 1), :]
    owner_sq = jnp.broadcast_to(owner_row, (LANES, LANES))
    sub, lane = iota((LANES, LANES), 0), iota((LANES, LANES), 1)
    same = (owner_sq.T == owner_sq) & (sub < lane)
    slot_row = jnp.sum(same.astype(jnp.int32), axis=0, keepdims=True)
    local = ids_ref[...] - column * LANES
    full = (8, LANES)
    dest = lane_gather(jnp.broadcast_to(owner_row, full), local)
    slot = lane_gather(jnp.broadcast_to(slot_row, full), local)
    pair = lane_gather(jnp.broadcast_to(pair_row, full), local)
    member = jnp.concatenate([(dest == o).astype(jnp.float32) for o in range(SHARDS)], axis=0)
    member = member.astype(jnp.bfloat16)
    before = (sub < lane).astype(jnp.bfloat16)
    in_row = jnp.dot(member, before, preferred_element_type=jnp.float32)
    above = ((sub // 8 == lane // 8) & (lane < sub)).astype(jnp.bfloat16)
    rows_above = jnp.dot(above, member, preferred_element_type=jnp.float32).astype(jnp.bfloat16)
    ones = jnp.ones((LANES, LANES), jnp.bfloat16)
    count = in_row + jnp.dot(rows_above, ones, preferred_element_type=jnp.float32)
    rank = jnp.zeros(full, jnp.float32)
    for o in range(SHARDS):
        rank = jnp.where(dest == o, count[o * 8 : (o + 1) * 8, :], rank)
    rank = rank.astype(jnp.int32)
    dest_ref[...] = dest
    rank_ref[...] = rank
    codes_t = codes_ref[...].astype(jnp.float32).T
    slot_f = (slot + 1).astype(jnp.float32)
    pair_f = (pair + 1).astype(jnp.float32)
    slot_line = jnp.concatenate([slot_f[k : k + 1, :] for k in range(8)], axis=1)
    pair_line = jnp.concatenate([pair_f[k : k + 1, :] for k in range(8)], axis=1)
    tail_row = iota((16, 1024), 0)
    tail = jnp.where(tail_row == 0, slot_line, jnp.where(tail_row == 1, pair_line, 0.0))
    left = jnp.concatenate([codes_t, tail], axis=0).astype(jnp.bfloat16)
    for o in range(SHARDS):
        key = jnp.where(dest == o, rank, -1)
        pick = jnp.concatenate(
            [
                (jnp.broadcast_to(key[k : k + 1, :], (LANES, LANES)) == sub).astype(jnp.float32)
                for k in range(8)
            ],
            axis=1,
        ).astype(jnp.bfloat16)
        block = lax.dot_general(
            left, pick, (((1,), (1,)), ((), ())), preferred_element_type=jnp.float32
        )
        send_ref[o] = block.astype(jnp.bfloat16)


EARLY = 6
SIDE = 256
PER = SIDE // CAP
CHUNKS = RECV // SIDE
GROUP = 16
GROUPS = SUBQ // GROUP


def group_rows(g):
    if isinstance(g, int):
        return slice(g * GROUP, (g + 1) * GROUP)
    return pl.ds(pl.multiple_of(g * GROUP, GROUP), GROUP)


def codes_of(got_ref, block, g):
    return got_ref[block, group_rows(g), :].astype(jnp.int32)


def add_norms(got_ref, norm_ref, block, g, total):
    part = group_rows(g)
    code = codes_of(got_ref, block, g)
    rest = code & 127
    low, high = norm_ref[part, :LANES], norm_ref[part, LANES:]
    return total + jnp.where(code < LANES, lane_gather(low, rest), lane_gather(high, rest))


def scale_of(total):
    norm = jnp.sum(total, axis=0, keepdims=True)
    return jnp.broadcast_to(lax.rsqrt(norm + norm_epsilon), (GROUP, LANES))


def decode_part(got_ref, table_ref, block, g, scale, ut_ref, lanes):
    code = codes_of(got_ref, block, g).astype(jnp.int16)
    rest = code & 127
    is_low = code < LANES
    for i in range(SUB):
        low, high = table_ref[g, i, :, :LANES], table_ref[g, i, :, LANES:]
        value = jnp.where(is_low, lane_gather(low, rest), lane_gather(high, rest))
        rows = group_rows(g * SUB + i)
        ut_ref[rows, lanes] = (value.astype(jnp.float32) * scale).astype(jnp.bfloat16)


def block_lanes(j):
    return slice(j * LANES, (j + 1) * LANES)


def key_row(got_ref, j, line):
    return got_ref[j, SUBQ : SUBQ + 16, :].astype(jnp.float32)[line : line + 1, :]


def spread_keys(got_ref, line, keys_ref):
    for j in range(SHARDS):
        key = key_row(got_ref, j, line)
        keys_ref[j * LANES : (j + 1) * LANES, :] = jnp.broadcast_to(key, (LANES, LANES)).T


def key_line(got_ref, j, line):
    key = key_row(got_ref, j, line)
    return jnp.broadcast_to(jnp.where(key == 0.0, -1.0, key), (8, LANES))


def tiles(x):
    return x.reshape(x.shape[0] // 8, 8, LANES)


def fold_lanes(row_best):
    return jnp.max(row_best.T, axis=0, keepdims=True)


def parts_of(rows):
    half = RECV // 2
    return [slice(r, min(r + half, rows)) for r in range(0, rows, half)]


def scales(got_ref, norm_ref, n):
    totals = [jnp.zeros((GROUP, LANES), jnp.float32)] * PER
    for g in range(GROUPS):
        totals = [add_norms(got_ref, norm_ref, n * PER + h, g, totals[h]) for h in range(PER)]
    return [scale_of(t) for t in totals]


def chunk_scores(n, parts, u_ref, ut, keys_ref, line_of, best_ref, fresh, own, between):
    cols = [jnp.full((8, LANES), -1.0, jnp.float32)] * PER
    for q, rows in enumerate(parts):
        scores = jnp.dot(u_ref[rows, :], ut[...], preferred_element_type=jnp.float32)
        between(q)
        key = tiles(keys_ref[rows, :])
        best = None if fresh(rows) else tiles(best_ref[rows, :])
        for h in range(PER):
            part = tiles(scores[:, h * LANES : (h + 1) * LANES])
            ok = key == line_of(h)[None]
            if own and rows.stop > n * SIDE:
                row = iota(part.shape, 0) * 8 + iota(part.shape, 1)
                ok = ok & (row != iota(part.shape, 2) + (h * LANES + n * SIDE - rows.start))
            part = jnp.where(ok, part, -1.0)
            best = part if best is None else jnp.maximum(best, part)
            cols[h] = jnp.maximum(cols[h], jnp.max(part, axis=0))
        best_ref[rows, :] = best.reshape(rows.stop - rows.start, LANES)
    return [jnp.max(c, axis=0, keepdims=True) for c in cols]


def own_piece(n, got_ref, u_ref, ut_ref, keys_ref, best_ref, out_ref, between):
    cols = chunk_scores(
        n,
        parts_of((n + 1) * SIDE),
        u_ref,
        ut_ref.at[:, n * SIDE : (n + 1) * SIDE],
        keys_ref,
        lambda h: key_line(got_ref, n * PER + h, 0),
        best_ref,
        lambda rows: False,
        True,
        between,
    )
    for h in range(PER):
        j = n * PER + h
        out_ref[j : j + 1, :] = cols[h]


def own_kernel(
    got_ref, table_ref, norm_ref, ut_ref, u_ref, slots_ref, pairs_ref, best_ref, out_ref
):
    eye = (iota((SIDE, SIDE), 0) == iota((SIDE, SIDE), 1)).astype(jnp.bfloat16)

    def decode_chunk(n, groups, scale):
        for g in groups:
            for h in range(PER):
                j = n * PER + h
                decode_part(got_ref, table_ref, j, g, scale[h], ut_ref, block_lanes(j))

    def turn_chunk(n):
        lanes = slice(n * SIDE, (n + 1) * SIDE)
        u_ref[lanes, :] = lax.dot_general(
            eye, ut_ref[:, lanes], (((1,), (1,)), ((), ())), preferred_element_type=jnp.float32
        ).astype(jnp.bfloat16)

    spread_keys(got_ref, 0, slots_ref)
    spread_keys(got_ref, 1, pairs_ref)
    best_ref[...] = jnp.full(best_ref.shape, -1.0, jnp.float32)
    out_ref[...] = jnp.full(out_ref.shape, -1.0, jnp.float32)
    decode_chunk(0, range(GROUPS), scales(got_ref, norm_ref, 0))
    turn_chunk(0)
    for n in range(1, CHUNKS + 1):
        if n < CHUNKS:
            scale = scales(got_ref, norm_ref, n)
            if n - 1 >= EARLY:
                decode_chunk(n, range(GROUPS), scale)
        if n - 1 < EARLY:
            count = len(parts_of(n * SIDE))

            def between(q):
                if n < CHUNKS:
                    decode_chunk(n, range(q * GROUPS // count, (q + 1) * GROUPS // count), scale)

            own_piece(n - 1, got_ref, u_ref, ut_ref, slots_ref, best_ref, out_ref, between)
        if n < CHUNKS:
            turn_chunk(n)


def within_kernel(got_ref, ut_ref, u_ref, slots_ref, best_in, out_in, out_ref, best_ref):
    out_ref[...] = out_in[...]
    best_ref[...] = best_in[...]
    for n in range(EARLY, CHUNKS):
        own_piece(n, got_ref, u_ref, ut_ref, slots_ref, best_ref, out_ref, lambda q: None)
    for j in range(SHARDS):
        row = fold_lanes(best_ref[j * LANES : (j + 1) * LANES, :])
        out_ref[j : j + 1, :] = jnp.maximum(out_ref[j : j + 1, :], row)


def across_kernel(pairs_ref, left_ref, table_ref, norm_ref, u_ref, *rest):
    last = len(rest) == 5
    if last:
        best_in, out_ref, row_ref, ut_a, ut_b = rest
        best_ref = best_in
    else:
        out_ref, best_ref, ut_a, ut_b = rest
    uts = (ut_a, ut_b)
    chunks = left_ref.shape[0] // PER
    parts = parts_of(RECV)

    def decode_chunk(n, groups, scale):
        for g in groups:
            for h in range(PER):
                j = n * PER + h
                decode_part(left_ref, table_ref, j, g, scale[h], uts[n % 2], block_lanes(h))

    decode_chunk(0, range(GROUPS), scales(left_ref, norm_ref, 0))
    for n in range(chunks):
        if n + 1 < chunks:
            scale = scales(left_ref, norm_ref, n + 1)

        def between(q):
            if n + 1 < chunks:
                count = len(parts)
                decode_chunk(n + 1, range(q * GROUPS // count, (q + 1) * GROUPS // count), scale)

        cols = chunk_scores(
            n,
            parts,
            u_ref,
            uts[n % 2],
            pairs_ref,
            lambda h: key_line(left_ref, n * PER + h, 0),
            best_ref,
            lambda rows: n == 0 and not last,
            False,
            between,
        )
        for h in range(PER):
            j = n * PER + h
            out_ref[j : j + 1, :] = cols[h]
    if last:
        for j in range(SHARDS):
            row_ref[j : j + 1, :] = fold_lanes(best_ref[j * LANES : (j + 1) * LANES, :])


def pick_kernel(got_ref, dest_ref, rank_ref, within_ref, near_ref):
    dest, rank = dest_ref[...], rank_ref[...]
    within = jnp.zeros((8, LANES), jnp.float32)
    near = within
    for o in range(SHARDS):
        here = dest == o
        first = jnp.broadcast_to(got_ref[o, 0:1, :], (8, LANES))
        second = jnp.broadcast_to(got_ref[o, 1:2, :], (8, LANES))
        within = jnp.where(here, lane_gather(first, rank), within)
        near = jnp.where(here, lane_gather(second, rank), near)
    within_ref[...] = within
    near_ref[...] = near


def kernel_call(body, shapes, count, scratch=(), name=None, flops=0):
    return pl.pallas_call(
        body,
        out_shape=shapes,
        in_specs=[VMEM] * count,
        out_specs=[VMEM] * len(shapes),
        scratch_shapes=list(scratch),
        compiler_params=pltpu.CompilerParams(vmem_limit_bytes=16 << 20),
        name=name,
        cost_estimate=pl.CostEstimate(flops=flops, bytes_accessed=1 << 20, transcendentals=0),
    )


def shape(dims, kind):
    return jax.ShapeDtypeStruct(dims, kind)


bf16, f32, i32 = jnp.bfloat16, jnp.float32, jnp.int32
K_ROUTE = (
    route_kernel,
    [shape((SHARDS, BLOCK, LANES), bf16), shape((8, LANES), i32), shape((8, LANES), i32)],
    4,
)
K_OWN = (
    own_kernel,
    [
        shape((EMB, RECV), bf16),
        shape((RECV, EMB), bf16),
        shape((RECV, LANES), f32),
        shape((RECV, LANES), f32),
        shape((RECV, LANES), f32),
        shape((SHARDS, LANES), f32),
    ],
    3,
)
UTS = [pltpu.VMEM((EMB, SIDE), bf16)] * 2
HALF = SHARDS // 2
K_FIRST = (across_kernel, [shape((HALF, LANES), f32), shape((RECV, LANES), f32)], 5, UTS)
K_SECOND = (across_kernel, [shape((HALF, LANES), f32), shape((SHARDS, LANES), f32)], 6, UTS)
K_WITHIN = (within_kernel, [shape((SHARDS, LANES), f32)], 6, [pltpu.VMEM((RECV, LANES), f32)])
K_PICK = (pick_kernel, [shape((8, LANES), f32), shape((8, LANES), f32)], 3)


def from_behind(x, axis, by):
    peers = lax.axis_size(axis)
    return lax.ppermute(x, axis, [(i, (i + by) % peers) for i in range(peers)])


def tables_of(codebook):
    turned = jnp.swapaxes(codebook, 1, 2)
    wide = turned.astype(f32)
    norms = jnp.sum(wide * wide, axis=1)
    return turned.reshape(GROUPS, GROUP, SUB, CODES_K).transpose(0, 2, 1, 3), norms


def scores_of(got, left, table, norms):
    ut, u, slots, pairs, best, early = kernel_call(*K_OWN, name="own", flops=8 << 30)(
        got, table, norms
    )
    cols_a, partial = kernel_call(*K_FIRST, name="first", flops=8 << 30)(
        pairs, left[0], table, norms, u
    )
    cols_b, from_left = kernel_call(*K_SECOND, name="second", flops=8 << 30)(
        pairs, left[1], table, norms, u, partial
    )

    def within():
        return kernel_call(*K_WITHIN, name="within", flops=4 << 30)(
            got, ut, u, slots, best, early
        )[0]

    return within, from_left, jnp.concatenate([cols_a, cols_b], axis=0)


def on_device(codes, cluster_ids, cluster_owner, left_pair, codebook):
    send, dest, rank = kernel_call(*K_ROUTE, name="route", flops=1 << 30)(
        codes,
        cluster_ids.reshape(8, LANES),
        cluster_owner.reshape(8, LANES),
        left_pair.reshape(8, LANES),
    )
    table, norms = tables_of(codebook)
    got = lax.all_to_all(send, "shard", split_axis=0, concat_axis=0, tiled=True)
    left = [from_behind(got[h * HALF : (h + 1) * HALF], "blk", 1) for h in range(2)]
    within, from_left, for_left = scores_of(got, left, table, norms)
    from_right = from_behind(for_left, "blk", -1)
    within = within()
    near = jnp.maximum(from_left, from_right)
    answers = jnp.stack([within, near], axis=1)
    back = lax.all_to_all(answers, "shard", split_axis=0, concat_axis=0, tiled=True)
    within_max, near_max = kernel_call(*K_PICK, name="pick")(back, dest, rank)
    return within_max.reshape(-1), near_max.reshape(-1)


def solution(mesh):
    in_specs = (P(("shard", "blk"), None), P(("shard", "blk")), P(), P(), P())
    out_specs = (P(("shard", "blk")), P(("shard", "blk")))
    return jax.shard_map(
        on_device, mesh=mesh, in_specs=in_specs, out_specs=out_specs, check_vma=False
    )
```

```python
import functools

import jax
import jax.numpy as jnp
from jax import lax
from jax.experimental import pallas as pl
from jax.experimental.pallas import tpu as pltpu
from jax.sharding import PartitionSpec as P

EMB = 1024
SUBQ = 128
SUB = 8
CODES_K = 256
CPD = 8
LANES = 128
SHARDS = 16
CAP = 128
RECV = SHARDS * CAP
BLOCK = SUBQ + 16
norm_epsilon = 1e-06

VMEM = pl.BlockSpec(memory_space=pltpu.VMEM)


def lane_gather(table, index):
    numbers = lax.GatherDimensionNumbers(
        offset_dims=(),
        collapsed_slice_dims=(1,),
        start_index_map=(1,),
        operand_batching_dims=(0,),
        start_indices_batching_dims=(0,),
    )
    return lax.gather(
        table,
        index[..., None],
        numbers,
        slice_sizes=(1, 1),
        mode=lax.GatherScatterMode.PROMISE_IN_BOUNDS,
    )


def iota(shape, axis):
    return lax.broadcasted_iota(jnp.int32, shape, axis)


def route_kernel(
    codes_hbm, ids_hbm, owner_hbm, pair_hbm, send_hbm, dest_ref, rank_ref,
    codes_ref, ids_ref, owner_ref, pair_ref, send_ref, in_sem, out_sem,
):
    loads = [
        pltpu.make_async_copy(src, dst, in_sem.at[k])
        for k, (src, dst) in enumerate(
            [
                (owner_hbm, owner_ref),
                (ids_hbm, ids_ref),
                (pair_hbm, pair_ref),
                (codes_hbm, codes_ref),
            ]
        )
    ]
    for load in loads:
        load.start()
    column = lax.axis_index("blk")
    full = (8, LANES)
    sub, lane = iota((LANES, LANES), 0), iota((LANES, LANES), 1)
    loads[0].wait()
    loads[1].wait()
    owner_row = owner_ref[pl.ds(column, 1), :]
    local = ids_ref[...] - column * LANES
    dest = lane_gather(jnp.broadcast_to(owner_row, full), local)
    member = jnp.concatenate([(dest == o).astype(jnp.float32) for o in range(SHARDS)], axis=0)
    member = member.astype(jnp.bfloat16)
    before = (sub < lane).astype(jnp.bfloat16)
    in_row = jnp.dot(member, before, preferred_element_type=jnp.float32)
    above = ((sub // 8 == lane // 8) & (lane < sub)).astype(jnp.bfloat16)
    rows_above = jnp.dot(above, member, preferred_element_type=jnp.float32)
    count = in_row + jnp.sum(rows_above, axis=1, keepdims=True)
    rank = jnp.zeros(full, jnp.float32)
    for o in range(SHARDS):
        rank = jnp.where(dest == o, count[o * 8 : (o + 1) * 8, :], rank)
    rank = rank.astype(jnp.int32)
    dest_ref[...] = dest
    rank_ref[...] = rank
    owner_sq = jnp.broadcast_to(owner_row, (LANES, LANES))
    same = (owner_sq.T == owner_sq) & (sub < lane)
    slot_row = jnp.sum(same.astype(jnp.int32), axis=0, keepdims=True)
    slot = lane_gather(jnp.broadcast_to(slot_row, full), local)
    loads[2].wait()
    pair_row = pair_ref[pl.ds(column, 1), :]
    pair = lane_gather(jnp.broadcast_to(pair_row, full), local)
    slot_f = (slot + 1).astype(jnp.float32)
    pair_f = (pair + 1).astype(jnp.float32)
    slot_line = jnp.concatenate([slot_f[k : k + 1, :] for k in range(8)], axis=1)
    pair_line = jnp.concatenate([pair_f[k : k + 1, :] for k in range(8)], axis=1)
    tail_row = iota((16, 1024), 0)
    tail = jnp.where(tail_row == 0, slot_line, jnp.where(tail_row == 1, pair_line, 0.0))
    loads[3].wait()
    codes_t = codes_ref[...].astype(jnp.float32).T
    left = jnp.concatenate([codes_t, tail], axis=0).astype(jnp.bfloat16)
    stores = []
    for o in range(0, SHARDS, OWNERS):
        picks = []
        for p in range(OWNERS):
            key = jnp.where(dest == o + p, rank, -1)
            pick = [
                (jnp.broadcast_to(key[k : k + 1, :], (LANES, LANES)) == sub).astype(jnp.float32)
                for k in range(8)
            ]
            picks.append(jnp.concatenate(pick, axis=1))
        pick = jnp.concatenate(picks, axis=0).astype(jnp.bfloat16)
        block = lax.dot_general(
            left, pick, (((1,), (1,)), ((), ())), preferred_element_type=jnp.float32
        ).astype(jnp.bfloat16)
        for p in range(OWNERS):
            send_ref[o + p] = block[:, p * LANES : (p + 1) * LANES]
        part = pl.ds(o, OWNERS)
        store = pltpu.make_async_copy(
            send_ref.at[part], send_hbm.at[part], out_sem.at[o // OWNERS]
        )
        store.start()
        stores.append(store)
    for store in stores:
        store.wait()


OWNERS = 2


EARLY = 5
SIDE = 256
PER = SIDE // CAP
CHUNKS = RECV // SIDE
GROUP = 16
GROUPS = SUBQ // GROUP


def group_rows(g):
    if isinstance(g, int):
        return slice(g * GROUP, (g + 1) * GROUP)
    return pl.ds(pl.multiple_of(g * GROUP, GROUP), GROUP)


def codes_of(got_ref, block, g):
    return got_ref[block, group_rows(g), :].astype(jnp.int32)


def add_norms(got_ref, norm_ref, block, g, total):
    part = group_rows(g)
    code = codes_of(got_ref, block, g)
    rest = code & 127
    low, high = norm_ref[part, :LANES], norm_ref[part, LANES:]
    return total + jnp.where(code < LANES, lane_gather(low, rest), lane_gather(high, rest))


def scale_of(total):
    norm = jnp.sum(total, axis=0, keepdims=True)
    return jnp.broadcast_to(lax.rsqrt(norm + norm_epsilon), (GROUP, LANES))


def decode_part(got_ref, table_ref, block, g, scale, ut_ref, lanes):
    code = codes_of(got_ref, block, g).astype(jnp.int16)
    rest = code & 127
    is_low = code < LANES
    for i in range(SUB):
        low, high = table_ref[g, i, :, :LANES], table_ref[g, i, :, LANES:]
        value = jnp.where(is_low, lane_gather(low, rest), lane_gather(high, rest))
        rows = group_rows(g * SUB + i)
        ut_ref[rows, lanes] = (value.astype(jnp.float32) * scale).astype(jnp.bfloat16)


def block_lanes(j):
    return slice(j * LANES, (j + 1) * LANES)


def key_row(got_ref, j, line):
    return got_ref[j, SUBQ : SUBQ + 16, :].astype(jnp.float32)[line : line + 1, :]


def spread_keys(got_ref, line, keys_ref):
    for j in range(SHARDS):
        key = key_row(got_ref, j, line)
        keys_ref[j * LANES : (j + 1) * LANES, :] = jnp.broadcast_to(key, (LANES, LANES)).T


def key_line(got_ref, j, line):
    key = key_row(got_ref, j, line)
    return jnp.broadcast_to(jnp.where(key == 0.0, -1.0, key), (8, LANES))


def tiles(x):
    return x.reshape(x.shape[0] // 8, 8, LANES)


def fold_lanes(row_best):
    return jnp.max(row_best.T, axis=0, keepdims=True)


def parts_of(rows):
    half = RECV // 2
    return [slice(r, min(r + half, rows)) for r in range(0, rows, half)]


def scales(got_ref, norm_ref, n):
    totals = [jnp.zeros((GROUP, LANES), jnp.float32)] * PER
    for g in range(GROUPS):
        totals = [add_norms(got_ref, norm_ref, n * PER + h, g, totals[h]) for h in range(PER)]
    return [scale_of(t) for t in totals]


def chunk_scores(n, parts, u_ref, ut, keys_ref, line_of, best_ref, fresh, own, between):
    cols = [jnp.full((8, LANES), -1.0, jnp.float32)] * PER
    for q, rows in enumerate(parts):
        scores = jnp.dot(u_ref[rows, :], ut[...], preferred_element_type=jnp.float32)
        between(q)
        key = tiles(keys_ref[rows, :])
        best = None if fresh(rows) else tiles(best_ref[rows, :])
        for h in range(PER):
            part = tiles(scores[:, h * LANES : (h + 1) * LANES])
            ok = key == line_of(h)[None]
            if own and rows.stop > n * SIDE:
                row = iota(part.shape, 0) * 8 + iota(part.shape, 1)
                ok = ok & (row != iota(part.shape, 2) + (h * LANES + n * SIDE - rows.start))
            part = jnp.where(ok, part, -1.0)
            best = part if best is None else jnp.maximum(best, part)
            cols[h] = jnp.maximum(cols[h], jnp.max(part, axis=0))
        best_ref[rows, :] = best.reshape(rows.stop - rows.start, LANES)
    return [jnp.max(c, axis=0, keepdims=True) for c in cols]


def own_piece(n, got_ref, u_ref, ut_ref, keys_ref, best_ref, out_ref, between):
    cols = chunk_scores(
        n,
        parts_of((n + 1) * SIDE),
        u_ref,
        ut_ref.at[:, n * SIDE : (n + 1) * SIDE],
        keys_ref,
        lambda h: key_line(got_ref, n * PER + h, 0),
        best_ref,
        lambda rows: False,
        True,
        between,
    )
    for h in range(PER):
        j = n * PER + h
        out_ref[j : j + 1, :] = cols[h]


def own_kernel(
    got_ref, table_ref, norm_ref, ut_ref, u_ref, slots_ref, pairs_ref, best_ref, out_ref
):
    eye = (iota((SIDE, SIDE), 0) == iota((SIDE, SIDE), 1)).astype(jnp.bfloat16)

    def decode_chunk(n, groups, scale):
        for g in groups:
            for h in range(PER):
                j = n * PER + h
                decode_part(got_ref, table_ref, j, g, scale[h], ut_ref, block_lanes(j))

    def turn_chunk(n):
        lanes = slice(n * SIDE, (n + 1) * SIDE)
        u_ref[lanes, :] = lax.dot_general(
            eye, ut_ref[:, lanes], (((1,), (1,)), ((), ())), preferred_element_type=jnp.float32
        ).astype(jnp.bfloat16)

    spread_keys(got_ref, 0, slots_ref)
    spread_keys(got_ref, 1, pairs_ref)
    best_ref[...] = jnp.full(best_ref.shape, -1.0, jnp.float32)
    out_ref[...] = jnp.full(out_ref.shape, -1.0, jnp.float32)
    decode_chunk(0, range(GROUPS), scales(got_ref, norm_ref, 0))
    turn_chunk(0)
    for n in range(1, CHUNKS + 1):
        if n < CHUNKS:
            scale = scales(got_ref, norm_ref, n)
            if n - 1 >= EARLY:
                decode_chunk(n, range(GROUPS), scale)
        if n - 1 < EARLY:
            count = len(parts_of(n * SIDE))

            def between(q):
                if n < CHUNKS:
                    decode_chunk(n, range(q * GROUPS // count, (q + 1) * GROUPS // count), scale)

            own_piece(n - 1, got_ref, u_ref, ut_ref, slots_ref, best_ref, out_ref, between)
        if n < CHUNKS:
            turn_chunk(n)


def within_kernel(got_ref, ut_ref, u_ref, slots_ref, best_in, out_in, out_ref, best_ref):
    out_ref[...] = out_in[...]
    best_ref[...] = best_in[...]
    for n in range(EARLY, CHUNKS):
        own_piece(n, got_ref, u_ref, ut_ref, slots_ref, best_ref, out_ref, lambda q: None)
    for j in range(SHARDS):
        row = fold_lanes(best_ref[j * LANES : (j + 1) * LANES, :])
        out_ref[j : j + 1, :] = jnp.maximum(out_ref[j : j + 1, :], row)


def across_kernel(pairs_ref, left_ref, table_ref, norm_ref, u_ref, *rest):
    last = len(rest) == 5
    if last:
        best_in, out_ref, row_ref, ut_a, ut_b = rest
        best_ref = best_in
    else:
        out_ref, best_ref, ut_a, ut_b = rest
    uts = (ut_a, ut_b)
    chunks = left_ref.shape[0] // PER
    parts = parts_of(RECV)

    def decode_chunk(n, groups, scale):
        for g in groups:
            for h in range(PER):
                j = n * PER + h
                decode_part(left_ref, table_ref, j, g, scale[h], uts[n % 2], block_lanes(h))

    decode_chunk(0, range(GROUPS), scales(left_ref, norm_ref, 0))
    for n in range(chunks):
        if n + 1 < chunks:
            scale = scales(left_ref, norm_ref, n + 1)

        def between(q):
            if n + 1 < chunks:
                count = len(parts)
                decode_chunk(n + 1, range(q * GROUPS // count, (q + 1) * GROUPS // count), scale)

        cols = chunk_scores(
            n,
            parts,
            u_ref,
            uts[n % 2],
            pairs_ref,
            lambda h: key_line(left_ref, n * PER + h, 0),
            best_ref,
            lambda rows: n == 0 and not last,
            False,
            between,
        )
        for h in range(PER):
            j = n * PER + h
            out_ref[j : j + 1, :] = cols[h]
    if last:
        for j in range(SHARDS):
            row_ref[j : j + 1, :] = fold_lanes(best_ref[j * LANES : (j + 1) * LANES, :])


def pick_kernel(got_ref, dest_ref, rank_ref, within_ref, near_ref):
    dest, rank = dest_ref[...], rank_ref[...]
    within = jnp.zeros((8, LANES), jnp.float32)
    near = within
    for o in range(SHARDS):
        here = dest == o
        first = jnp.broadcast_to(got_ref[o, 0:1, :], (8, LANES))
        second = jnp.broadcast_to(got_ref[o, 1:2, :], (8, LANES))
        within = jnp.where(here, lane_gather(first, rank), within)
        near = jnp.where(here, lane_gather(second, rank), near)
    within_ref[...] = within
    near_ref[...] = near


def kernel_call(body, shapes, count, scratch=(), name=None, flops=0):
    return pl.pallas_call(
        body,
        out_shape=shapes,
        in_specs=[VMEM] * count,
        out_specs=[VMEM] * len(shapes),
        scratch_shapes=list(scratch),
        compiler_params=pltpu.CompilerParams(vmem_limit_bytes=16 << 20),
        name=name,
        cost_estimate=pl.CostEstimate(flops=flops, bytes_accessed=1 << 20, transcendentals=0),
    )


def shape(dims, kind):
    return jax.ShapeDtypeStruct(dims, kind)


bf16, f32, i32 = jnp.bfloat16, jnp.float32, jnp.int32
K_OWN = (
    own_kernel,
    [
        shape((EMB, RECV), bf16),
        shape((RECV, EMB), bf16),
        shape((RECV, LANES), f32),
        shape((RECV, LANES), f32),
        shape((RECV, LANES), f32),
        shape((SHARDS, LANES), f32),
    ],
    3,
)
UTS = [pltpu.VMEM((EMB, SIDE), bf16)] * 2
HALF = SHARDS // 2
K_FIRST = (across_kernel, [shape((HALF, LANES), f32), shape((RECV, LANES), f32)], 5, UTS)
K_SECOND = (across_kernel, [shape((HALF, LANES), f32), shape((SHARDS, LANES), f32)], 6, UTS)
K_WITHIN = (within_kernel, [shape((SHARDS, LANES), f32)], 6, [pltpu.VMEM((RECV, LANES), f32)])
K_PICK = (pick_kernel, [shape((8, LANES), f32), shape((8, LANES), f32)], 3)


def route_call(*operands):
    small = pltpu.VMEM((8, LANES), i32)
    outside = pl.BlockSpec(memory_space=pltpu.HBM)
    return pl.pallas_call(
        route_kernel,
        out_shape=[
            shape((SHARDS, BLOCK, LANES), bf16),
            shape((8, LANES), i32),
            shape((8, LANES), i32),
        ],
        in_specs=[outside] * 4,
        out_specs=[outside, VMEM, VMEM],
        scratch_shapes=[
            pltpu.VMEM((SHARDS * 64, LANES), i32),
            small,
            small,
            small,
            pltpu.VMEM((SHARDS, BLOCK, LANES), bf16),
            pltpu.SemaphoreType.DMA((4,)),
            pltpu.SemaphoreType.DMA((SHARDS // OWNERS,)),
        ],
        compiler_params=pltpu.CompilerParams(vmem_limit_bytes=16 << 20),
        name="route",
    )(*[pltpu.with_memory_space_constraint(x, pltpu.HBM) for x in operands])


def from_behind(x, axis, by):
    peers = lax.axis_size(axis)
    return lax.ppermute(x, axis, [(i, (i + by) % peers) for i in range(peers)])


def tables_of(codebook):
    turned = jnp.swapaxes(codebook, 1, 2)
    wide = turned.astype(f32)
    norms = jnp.sum(wide * wide, axis=1)
    return turned.reshape(GROUPS, GROUP, SUB, CODES_K).transpose(0, 2, 1, 3), norms


def scores_of(got, left, table, norms):
    ut, u, slots, pairs, best, early = kernel_call(*K_OWN, name="own", flops=8 << 30)(
        got, table, norms
    )
    cols_a, partial = kernel_call(*K_FIRST, name="first", flops=8 << 30)(
        pairs, left[0], table, norms, u
    )
    cols_b, from_left = kernel_call(*K_SECOND, name="second", flops=8 << 30)(
        pairs, left[1], table, norms, u, partial
    )

    def within():
        return kernel_call(*K_WITHIN, name="within", flops=4 << 30)(
            got, ut, u, slots, best, early
        )[0]

    return within, from_left, jnp.concatenate([cols_a, cols_b], axis=0)


def on_device(codes, cluster_ids, cluster_owner, left_pair, codebook):
    send, dest, rank = route_call(
        codes,
        cluster_ids.reshape(8, LANES),
        cluster_owner.reshape(8, LANES),
        left_pair.reshape(8, LANES),
    )
    table, norms = tables_of(codebook)
    got = lax.all_to_all(send, "shard", split_axis=0, concat_axis=0, tiled=True)
    left = [from_behind(got[h * HALF : (h + 1) * HALF], "blk", 1) for h in range(2)]
    within, from_left, for_left = scores_of(got, left, table, norms)
    from_right = from_behind(for_left, "blk", -1)
    within = within()
    near = jnp.maximum(from_left, from_right)
    answers = jnp.stack([within, near], axis=1)
    back = lax.all_to_all(answers, "shard", split_axis=0, concat_axis=0, tiled=True)
    within_max, near_max = kernel_call(*K_PICK, name="pick")(back, dest, rank)
    return within_max.reshape(-1), near_max.reshape(-1)


def solution(mesh):
    in_specs = (P(("shard", "blk"), None), P(("shard", "blk")), P(), P(), P())
    out_specs = (P(("shard", "blk")), P(("shard", "blk")))
    return jax.shard_map(
        on_device, mesh=mesh, in_specs=in_specs, out_specs=out_specs, check_vma=False
    )
```

```python
import functools

import jax
import jax.numpy as jnp
from jax import lax
from jax.experimental import pallas as pl
from jax.experimental.pallas import tpu as pltpu
from jax.sharding import PartitionSpec as P

EMB = 1024
SUBQ = 128
SUB = 8
CODES_K = 256
CPD = 8
LANES = 128
SHARDS = 16
CAP = 128
RECV = SHARDS * CAP
BLOCK = SUBQ + 16
norm_epsilon = 1e-06

VMEM = pl.BlockSpec(memory_space=pltpu.VMEM)


def lane_gather(table, index):
    numbers = lax.GatherDimensionNumbers(
        offset_dims=(),
        collapsed_slice_dims=(1,),
        start_index_map=(1,),
        operand_batching_dims=(0,),
        start_indices_batching_dims=(0,),
    )
    return lax.gather(
        table,
        index[..., None],
        numbers,
        slice_sizes=(1, 1),
        mode=lax.GatherScatterMode.PROMISE_IN_BOUNDS,
    )


def iota(shape, axis):
    return lax.broadcasted_iota(jnp.int32, shape, axis)


def route_kernel(
    codes_hbm, ids_hbm, owner_hbm, pair_hbm, send_hbm, dest_ref, rank_ref,
    codes_ref, ids_ref, owner_ref, pair_ref, send_ref, in_sem, out_sem,
):
    loads = [
        pltpu.make_async_copy(src, dst, in_sem.at[k])
        for k, (src, dst) in enumerate(
            [
                (owner_hbm, owner_ref),
                (ids_hbm, ids_ref),
                (pair_hbm, pair_ref),
                (codes_hbm, codes_ref),
            ]
        )
    ]
    for load in loads:
        load.start()
    column = lax.axis_index("blk")
    full = (8, LANES)
    sub, lane = iota((LANES, LANES), 0), iota((LANES, LANES), 1)
    loads[0].wait()
    loads[1].wait()
    owner_row = owner_ref[pl.ds(column, 1), :]
    local = ids_ref[...] - column * LANES
    dest = lane_gather(jnp.broadcast_to(owner_row, full), local)
    member = jnp.concatenate([(dest == o).astype(jnp.float32) for o in range(SHARDS)], axis=0)
    member = member.astype(jnp.bfloat16)
    before = (sub < lane).astype(jnp.bfloat16)
    in_row = jnp.dot(member, before, preferred_element_type=jnp.float32)
    above = ((sub // 8 == lane // 8) & (lane < sub)).astype(jnp.bfloat16)
    rows_above = jnp.dot(above, member, preferred_element_type=jnp.float32)
    count = in_row + jnp.sum(rows_above, axis=1, keepdims=True)
    rank = jnp.zeros(full, jnp.float32)
    for o in range(SHARDS):
        rank = jnp.where(dest == o, count[o * 8 : (o + 1) * 8, :], rank)
    rank = rank.astype(jnp.int32)
    dest_ref[...] = dest
    rank_ref[...] = rank
    owner_sq = jnp.broadcast_to(owner_row, (LANES, LANES))
    same = (owner_sq.T == owner_sq) & (sub < lane)
    slot_row = jnp.sum(same.astype(jnp.int32), axis=0, keepdims=True)
    slot = lane_gather(jnp.broadcast_to(slot_row, full), local)
    loads[2].wait()
    pair_row = pair_ref[pl.ds(column, 1), :]
    pair = lane_gather(jnp.broadcast_to(pair_row, full), local)
    slot_f = (slot + 1).astype(jnp.float32)
    pair_f = (pair + 1).astype(jnp.float32)
    slot_line = jnp.concatenate([slot_f[k : k + 1, :] for k in range(8)], axis=1)
    pair_line = jnp.concatenate([pair_f[k : k + 1, :] for k in range(8)], axis=1)
    tail_row = iota((16, 1024), 0)
    tail = jnp.where(tail_row == 0, slot_line, jnp.where(tail_row == 1, pair_line, 0.0))
    loads[3].wait()
    codes_t = codes_ref[...].astype(jnp.float32).T
    left = jnp.concatenate([codes_t, tail], axis=0).astype(jnp.bfloat16)
    stores = []
    for o in range(0, SHARDS, OWNERS):
        picks = []
        for p in range(OWNERS):
            key = jnp.where(dest == o + p, rank, -1)
            pick = [
                (jnp.broadcast_to(key[k : k + 1, :], (LANES, LANES)) == sub).astype(jnp.float32)
                for k in range(8)
            ]
            picks.append(jnp.concatenate(pick, axis=1))
        pick = jnp.concatenate(picks, axis=0).astype(jnp.bfloat16)
        block = lax.dot_general(
            left, pick, (((1,), (1,)), ((), ())), preferred_element_type=jnp.float32
        ).astype(jnp.bfloat16)
        for p in range(OWNERS):
            send_ref[o + p] = block[:, p * LANES : (p + 1) * LANES]
        part = pl.ds(o, OWNERS)
        store = pltpu.make_async_copy(
            send_ref.at[part], send_hbm.at[part], out_sem.at[o // OWNERS]
        )
        store.start()
        stores.append(store)
    for store in stores:
        store.wait()


OWNERS = 2


EARLY = 5
SIDE = 256
PER = SIDE // CAP
CHUNKS = RECV // SIDE
GROUP = 16
GROUPS = SUBQ // GROUP


def group_rows(g):
    if isinstance(g, int):
        return slice(g * GROUP, (g + 1) * GROUP)
    return pl.ds(pl.multiple_of(g * GROUP, GROUP), GROUP)


def codes_of(got_ref, block, g):
    return got_ref[block, group_rows(g), :].astype(jnp.int32)


def add_norms(got_ref, norm_ref, block, g, total):
    part = group_rows(g)
    code = codes_of(got_ref, block, g)
    rest = code & 127
    low, high = norm_ref[part, :LANES], norm_ref[part, LANES:]
    return total + jnp.where(code < LANES, lane_gather(low, rest), lane_gather(high, rest))


def scale_of(total):
    norm = jnp.sum(total, axis=0, keepdims=True)
    return jnp.broadcast_to(lax.rsqrt(norm + norm_epsilon), (GROUP, LANES))


def decode_part(got_ref, table_ref, block, g, scale, ut_ref, lanes):
    code = codes_of(got_ref, block, g).astype(jnp.int16)
    rest = code & 127
    is_low = code < LANES
    for i in range(SUB):
        low, high = table_ref[g, i, :, :LANES], table_ref[g, i, :, LANES:]
        value = jnp.where(is_low, lane_gather(low, rest), lane_gather(high, rest))
        rows = group_rows(g * SUB + i)
        ut_ref[rows, lanes] = (value.astype(jnp.float32) * scale).astype(jnp.bfloat16)


def block_lanes(j):
    return slice(j * LANES, (j + 1) * LANES)


def key_row(got_ref, j, line):
    return got_ref[j, SUBQ : SUBQ + 16, :].astype(jnp.float32)[line : line + 1, :]


def spread_keys(got_ref, line, keys_ref):
    for j in range(SHARDS):
        key = key_row(got_ref, j, line)
        keys_ref[j * LANES : (j + 1) * LANES, :] = jnp.broadcast_to(key, (LANES, LANES)).T


def key_line(got_ref, j, line):
    key = key_row(got_ref, j, line)
    return jnp.broadcast_to(jnp.where(key == 0.0, -1.0, key), (8, LANES))


def tiles(x):
    return x.reshape(x.shape[0] // 8, 8, LANES)


def fold_lanes(row_best):
    return jnp.max(row_best.T, axis=0, keepdims=True)


def parts_of(rows):
    half = RECV // 2
    return [slice(r, min(r + half, rows)) for r in range(0, rows, half)]


def scales(got_ref, norm_ref, n):
    totals = [jnp.zeros((GROUP, LANES), jnp.float32)] * PER
    for g in range(GROUPS):
        totals = [add_norms(got_ref, norm_ref, n * PER + h, g, totals[h]) for h in range(PER)]
    return [scale_of(t) for t in totals]


def chunk_scores(n, parts, u_ref, ut, keys_ref, line_of, best_ref, old_ref, own, between):
    cols = [jnp.full((8, LANES), -1.0, jnp.float32)] * PER
    for q, rows in enumerate(parts):
        scores = jnp.dot(u_ref[rows, :], ut[...], preferred_element_type=jnp.float32)
        between(q)
        key = tiles(keys_ref[rows, :])
        best = None if old_ref is None else tiles(old_ref[rows, :])
        for h in range(PER):
            part = tiles(scores[:, h * LANES : (h + 1) * LANES])
            ok = key == line_of(h)[None]
            if own and rows.stop > n * SIDE:
                row = iota(part.shape, 0) * 8 + iota(part.shape, 1)
                ok = ok & (row != iota(part.shape, 2) + (h * LANES + n * SIDE - rows.start))
            part = jnp.where(ok, part, -1.0)
            best = part if best is None else jnp.maximum(best, part)
            cols[h] = jnp.maximum(cols[h], jnp.max(part, axis=0))
        best_ref[rows, :] = best.reshape(rows.stop - rows.start, LANES)
    return [jnp.max(c, axis=0, keepdims=True) for c in cols]


def own_piece(n, got_ref, u_ref, ut_ref, keys_ref, best_ref, out_ref, between, alone=False):
    cols = chunk_scores(
        n,
        parts_of((n + 1) * SIDE),
        u_ref,
        ut_ref.at[:, n * SIDE : (n + 1) * SIDE],
        keys_ref,
        lambda h: key_line(got_ref, n * PER + h, 0),
        best_ref,
        None if alone else best_ref,
        True,
        between,
    )
    for h in range(PER):
        j = h if alone else n * PER + h
        out_ref[j : j + 1, :] = cols[h]


def own_kernel(
    got_ref, table_ref, norm_ref, ut_ref, u_ref, slots_ref, pairs_ref, best_ref, out_ref
):
    eye = (iota((SIDE, SIDE), 0) == iota((SIDE, SIDE), 1)).astype(jnp.bfloat16)

    def decode_chunk(n, groups, scale):
        for g in groups:
            for h in range(PER):
                j = n * PER + h
                decode_part(got_ref, table_ref, j, g, scale[h], ut_ref, block_lanes(j))

    def turn_chunk(n):
        lanes = slice(n * SIDE, (n + 1) * SIDE)
        u_ref[lanes, :] = lax.dot_general(
            eye, ut_ref[:, lanes], (((1,), (1,)), ((), ())), preferred_element_type=jnp.float32
        ).astype(jnp.bfloat16)

    spread_keys(got_ref, 0, slots_ref)
    spread_keys(got_ref, 1, pairs_ref)
    best_ref[...] = jnp.full(best_ref.shape, -1.0, jnp.float32)
    out_ref[...] = jnp.full(out_ref.shape, -1.0, jnp.float32)
    decode_chunk(0, range(GROUPS), scales(got_ref, norm_ref, 0))
    turn_chunk(0)
    for n in range(1, CHUNKS + 1):
        if n < CHUNKS:
            scale = scales(got_ref, norm_ref, n)
            if n - 1 >= EARLY:
                decode_chunk(n, range(GROUPS), scale)
        if n - 1 < EARLY:
            count = len(parts_of(n * SIDE))

            def between(q):
                if n < CHUNKS:
                    decode_chunk(n, range(q * GROUPS // count, (q + 1) * GROUPS // count), scale)

            own_piece(n - 1, got_ref, u_ref, ut_ref, slots_ref, best_ref, out_ref, between)
        if n < CHUNKS:
            turn_chunk(n)


def fold_rows(best_ref, out_ref, rows, join):
    for j in range(rows.start // LANES, rows.stop // LANES):
        row = fold_lanes(best_ref[j * LANES : (j + 1) * LANES, :])
        if join:
            row = jnp.maximum(out_ref[j : j + 1, :], row)
        out_ref[j : j + 1, :] = row


def within_kernel(
    got_ref, ut_ref, u_ref, slots_ref, best_in, early_in, best_more, more_in, out_ref, best_ref
):
    out_ref[...] = early_in[...]
    out_ref[EARLY * PER : (EARLY + 1) * PER, :] = more_in[...]
    rows = (EARLY + 1) * SIDE
    best_ref[:rows, :] = jnp.maximum(best_in[:rows, :], best_more[...])
    best_ref[rows:, :] = best_in[rows:, :]
    parts = parts_of(RECV)

    def between(n, q):
        if n == CHUNKS - 1 and q > 0:
            fold_rows(best_ref, out_ref, parts[q - 1], True)

    for n in range(EARLY + 1, CHUNKS):
        own_piece(
            n, got_ref, u_ref, ut_ref, slots_ref, best_ref, out_ref, lambda q: between(n, q)
        )
    fold_rows(best_ref, out_ref, parts[-1], True)


def decode_left(left_ref, table_ref, j, groups, scale, ut):
    for g in groups:
        for h in range(PER):
            decode_part(left_ref, table_ref, j + h, g, scale[h], ut, block_lanes(h))


def share(groups, q, count):
    return range(q * groups // count, (q + 1) * groups // count)


def left_scores(left_ref, j, pairs_ref, u_ref, ut, best_ref, old_ref, out_ref, row, between):
    cols = chunk_scores(
        0,
        parts_of(RECV),
        u_ref,
        ut,
        pairs_ref,
        lambda h: key_line(left_ref, j + h, 0),
        best_ref,
        old_ref,
        False,
        between,
    )
    for h in range(PER):
        out_ref[row + h : row + h + 1, :] = cols[h]


def first_kernel(
    pairs_ref, left_ref, table_ref, norm_ref, u_ref, got_ref, own_ref, slots_ref,
    out_ref, best_ref, ut_b, best_more, more_ref, ut_a,
):
    uts = (ut_a, ut_b)
    scale = scales(left_ref, norm_ref, 0)
    count = len(parts_of((EARLY + 1) * SIDE))
    own_piece(
        EARLY,
        got_ref,
        u_ref,
        own_ref,
        slots_ref,
        best_more,
        more_ref,
        lambda q: decode_left(left_ref, table_ref, 0, share(GROUPS, q, count), scale, ut_a),
        True,
    )
    for n in range(HALF // PER - 1):
        j = (n + 1) * PER
        scale = scales(left_ref, norm_ref, n + 1)
        left_scores(
            left_ref,
            n * PER,
            pairs_ref,
            u_ref,
            uts[n % 2],
            best_ref,
            best_ref if n else None,
            out_ref,
            n * PER,
            lambda q: decode_left(
                left_ref, table_ref, j, share(GROUPS, q, 2), scale, uts[(n + 1) % 2]
            ),
        )


def second_kernel(
    pairs_ref, before_ref, left_ref, table_ref, norm_ref, u_ref, best_in, ut_in,
    out_ref, row_ref, ut_a, ut_b, best_ref,
):
    uts = (ut_in, ut_a, ut_b)
    parts = parts_of(RECV)
    chunks = HALF // PER
    for n in range(chunks + 1):
        now = uts[0] if n == 0 else uts[1 + (n - 1) % 2]
        scale = scales(left_ref, norm_ref, n) if n < chunks else None

        def between(q):
            if n < chunks:
                decode_left(
                    left_ref, table_ref, n * PER, share(GROUPS, q, 2), scale, uts[1 + n % 2]
                )
            elif q > 0:
                fold_rows(best_ref, row_ref, parts[q - 1], False)

        left_scores(
            left_ref if n else before_ref,
            (n - 1) * PER if n else HALF - PER,
            pairs_ref,
            u_ref,
            now,
            best_ref,
            best_ref if n else best_in,
            out_ref,
            n * PER,
            between,
        )
    fold_rows(best_ref, row_ref, parts[-1], False)


def pick_kernel(got_ref, dest_ref, rank_ref, within_ref, near_ref):
    dest, rank = dest_ref[...], rank_ref[...]
    within = jnp.zeros((8, LANES), jnp.float32)
    near = within
    for o in range(SHARDS):
        here = dest == o
        first = jnp.broadcast_to(got_ref[o, 0:1, :], (8, LANES))
        second = jnp.broadcast_to(got_ref[o, 1:2, :], (8, LANES))
        within = jnp.where(here, lane_gather(first, rank), within)
        near = jnp.where(here, lane_gather(second, rank), near)
    within_ref[...] = within
    near_ref[...] = near


def kernel_call(body, shapes, count, scratch=(), name=None, flops=0):
    return pl.pallas_call(
        body,
        out_shape=shapes,
        in_specs=[VMEM] * count,
        out_specs=[VMEM] * len(shapes),
        scratch_shapes=list(scratch),
        compiler_params=pltpu.CompilerParams(vmem_limit_bytes=16 << 20),
        name=name,
        cost_estimate=pl.CostEstimate(flops=flops, bytes_accessed=1 << 20, transcendentals=0),
    )


def shape(dims, kind):
    return jax.ShapeDtypeStruct(dims, kind)


bf16, f32, i32 = jnp.bfloat16, jnp.float32, jnp.int32
K_OWN = (
    own_kernel,
    [
        shape((EMB, RECV), bf16),
        shape((RECV, EMB), bf16),
        shape((RECV, LANES), f32),
        shape((RECV, LANES), f32),
        shape((RECV, LANES), f32),
        shape((SHARDS, LANES), f32),
    ],
    3,
)
UT = pltpu.VMEM((EMB, SIDE), bf16)
BEST = pltpu.VMEM((RECV, LANES), f32)
HALF = SHARDS // 2
K_FIRST = (
    first_kernel,
    [
        shape((HALF - PER, LANES), f32),
        shape((RECV, LANES), f32),
        shape((EMB, SIDE), bf16),
        shape(((EARLY + 1) * SIDE, LANES), f32),
        shape((PER, LANES), f32),
    ],
    8,
    [UT],
)
K_SECOND = (
    second_kernel,
    [shape((HALF + PER, LANES), f32), shape((SHARDS, LANES), f32)],
    8,
    [UT, UT, BEST],
)
K_WITHIN = (within_kernel, [shape((SHARDS, LANES), f32)], 8, [BEST])
K_PICK = (pick_kernel, [shape((8, LANES), f32), shape((8, LANES), f32)], 3)


def route_call(*operands):
    small = pltpu.VMEM((8, LANES), i32)
    outside = pl.BlockSpec(memory_space=pltpu.HBM)
    return pl.pallas_call(
        route_kernel,
        out_shape=[
            shape((SHARDS, BLOCK, LANES), bf16),
            shape((8, LANES), i32),
            shape((8, LANES), i32),
        ],
        in_specs=[outside] * 4,
        out_specs=[outside, VMEM, VMEM],
        scratch_shapes=[
            pltpu.VMEM((SHARDS * 64, LANES), i32),
            small,
            small,
            small,
            pltpu.VMEM((SHARDS, BLOCK, LANES), bf16),
            pltpu.SemaphoreType.DMA((4,)),
            pltpu.SemaphoreType.DMA((SHARDS // OWNERS,)),
        ],
        compiler_params=pltpu.CompilerParams(vmem_limit_bytes=16 << 20),
        name="route",
    )(*[pltpu.with_memory_space_constraint(x, pltpu.HBM) for x in operands])


def from_behind(x, axis, by):
    peers = lax.axis_size(axis)
    return lax.ppermute(x, axis, [(i, (i + by) % peers) for i in range(peers)])


def tables_of(codebook):
    turned = jnp.swapaxes(codebook, 1, 2)
    wide = turned.astype(f32)
    norms = jnp.sum(wide * wide, axis=1)
    return turned.reshape(GROUPS, GROUP, SUB, CODES_K).transpose(0, 2, 1, 3), norms


def scores_of(got, left, table, norms):
    ut, u, slots, pairs, best, early = kernel_call(*K_OWN, name="own", flops=8 << 30)(
        got, table, norms
    )
    cols_a, partial, ut_last, best_more, more = kernel_call(
        *K_FIRST, name="first", flops=8 << 30
    )(pairs, left[0], table, norms, u, got, ut, slots)
    cols_b, from_left = kernel_call(*K_SECOND, name="second", flops=8 << 30)(
        pairs, left[0], left[1], table, norms, u, partial, ut_last
    )

    def within():
        return kernel_call(*K_WITHIN, name="within", flops=4 << 30)(
            got, ut, u, slots, best, early, best_more, more
        )[0]

    return within, from_left, jnp.concatenate([cols_a, cols_b], axis=0)


def on_device(codes, cluster_ids, cluster_owner, left_pair, codebook):
    send, dest, rank = route_call(
        codes,
        cluster_ids.reshape(8, LANES),
        cluster_owner.reshape(8, LANES),
        left_pair.reshape(8, LANES),
    )
    table, norms = tables_of(codebook)
    got = lax.all_to_all(send, "shard", split_axis=0, concat_axis=0, tiled=True)
    left = [from_behind(got[h * HALF : (h + 1) * HALF], "blk", 1) for h in range(2)]
    within, from_left, for_left = scores_of(got, left, table, norms)
    from_right = from_behind(for_left, "blk", -1)
    within = within()
    near = jnp.maximum(from_left, from_right)
    answers = jnp.stack([within, near], axis=1)
    back = lax.all_to_all(answers, "shard", split_axis=0, concat_axis=0, tiled=True)
    within_max, near_max = kernel_call(*K_PICK, name="pick")(back, dest, rank)
    return within_max.reshape(-1), near_max.reshape(-1)


def solution(mesh):
    in_specs = (P(("shard", "blk"), None), P(("shard", "blk")), P(), P(), P())
    out_specs = (P(("shard", "blk")), P(("shard", "blk")))
    return jax.shard_map(
        on_device, mesh=mesh, in_specs=in_specs, out_specs=out_specs, check_vma=False
    )
```

```python
import functools

import jax
import jax.numpy as jnp
from jax import lax
from jax.experimental import pallas as pl
from jax.experimental.pallas import tpu as pltpu
from jax.sharding import PartitionSpec as P

EMB = 1024
SUBQ = 128
SUB = 8
CODES_K = 256
CPD = 8
LANES = 128
SHARDS = 16
CAP = 128
RECV = SHARDS * CAP
BLOCK = SUBQ + 16
norm_epsilon = 1e-06

VMEM = pl.BlockSpec(memory_space=pltpu.VMEM)


def lane_gather(table, index):
    numbers = lax.GatherDimensionNumbers(
        offset_dims=(),
        collapsed_slice_dims=(1,),
        start_index_map=(1,),
        operand_batching_dims=(0,),
        start_indices_batching_dims=(0,),
    )
    return lax.gather(
        table,
        index[..., None],
        numbers,
        slice_sizes=(1, 1),
        mode=lax.GatherScatterMode.PROMISE_IN_BOUNDS,
    )


def iota(shape, axis):
    return lax.broadcasted_iota(jnp.int32, shape, axis)


def route_kernel(
    codes_hbm, ids_hbm, owner_hbm, pair_hbm, send_hbm, dest_ref, rank_ref,
    codes_ref, ids_ref, owner_ref, pair_ref, send_ref, in_sem, out_sem,
):
    loads = [
        pltpu.make_async_copy(src, dst, in_sem.at[k])
        for k, (src, dst) in enumerate(
            [
                (owner_hbm, owner_ref),
                (ids_hbm, ids_ref),
                (pair_hbm, pair_ref),
                (codes_hbm, codes_ref),
            ]
        )
    ]
    for load in loads:
        load.start()
    column = lax.axis_index("blk")
    full = (8, LANES)
    sub, lane = iota((LANES, LANES), 0), iota((LANES, LANES), 1)
    loads[0].wait()
    loads[1].wait()
    owner_row = owner_ref[pl.ds(column, 1), :]
    local = ids_ref[...] - column * LANES
    dest = lane_gather(jnp.broadcast_to(owner_row, full), local)
    member = jnp.concatenate([(dest == o).astype(jnp.float32) for o in range(SHARDS)], axis=0)
    member = member.astype(jnp.bfloat16)
    before = (sub < lane).astype(jnp.bfloat16)
    in_row = jnp.dot(member, before, preferred_element_type=jnp.float32)
    above = ((sub // 8 == lane // 8) & (lane < sub)).astype(jnp.bfloat16)
    rows_above = jnp.dot(above, member, preferred_element_type=jnp.float32)
    count = in_row + jnp.sum(rows_above, axis=1, keepdims=True)
    rank = jnp.zeros(full, jnp.float32)
    for o in range(SHARDS):
        rank = jnp.where(dest == o, count[o * 8 : (o + 1) * 8, :], rank)
    rank = rank.astype(jnp.int32)
    dest_ref[...] = dest
    rank_ref[...] = rank
    owner_sq = jnp.broadcast_to(owner_row, (LANES, LANES))
    same = (owner_sq.T == owner_sq) & (sub < lane)
    slot_row = jnp.sum(same.astype(jnp.int32), axis=0, keepdims=True)
    slot = lane_gather(jnp.broadcast_to(slot_row, full), local)
    loads[2].wait()
    pair_row = pair_ref[pl.ds(column, 1), :]
    pair = lane_gather(jnp.broadcast_to(pair_row, full), local)
    slot_f = (slot + 1).astype(jnp.float32)
    pair_f = (pair + 1).astype(jnp.float32)
    slot_line = jnp.concatenate([slot_f[k : k + 1, :] for k in range(8)], axis=1)
    pair_line = jnp.concatenate([pair_f[k : k + 1, :] for k in range(8)], axis=1)
    tail_row = iota((16, 1024), 0)
    tail = jnp.where(tail_row == 0, slot_line, jnp.where(tail_row == 1, pair_line, 0.0))
    loads[3].wait()
    codes_t = codes_ref[...].astype(jnp.float32).T
    left = jnp.concatenate([codes_t, tail], axis=0).astype(jnp.bfloat16)
    stores = []
    for o in range(0, SHARDS, OWNERS):
        picks = []
        for p in range(OWNERS):
            key = jnp.where(dest == o + p, rank, -1)
            pick = [
                (jnp.broadcast_to(key[k : k + 1, :], (LANES, LANES)) == sub).astype(jnp.float32)
                for k in range(8)
            ]
            picks.append(jnp.concatenate(pick, axis=1))
        pick = jnp.concatenate(picks, axis=0).astype(jnp.bfloat16)
        block = lax.dot_general(
            left, pick, (((1,), (1,)), ((), ())), preferred_element_type=jnp.float32
        ).astype(jnp.bfloat16)
        for p in range(OWNERS):
            send_ref[o + p] = block[:, p * LANES : (p + 1) * LANES]
        part = pl.ds(o, OWNERS)
        store = pltpu.make_async_copy(
            send_ref.at[part], send_hbm.at[part], out_sem.at[o // OWNERS]
        )
        store.start()
        stores.append(store)
    for store in stores:
        store.wait()


OWNERS = 2


FOLD = 6
EARLY = 5
SIDE = 256
PER = SIDE // CAP
CHUNKS = RECV // SIDE
GROUP = 16
GROUPS = SUBQ // GROUP


def group_rows(g):
    if isinstance(g, int):
        return slice(g * GROUP, (g + 1) * GROUP)
    return pl.ds(pl.multiple_of(g * GROUP, GROUP), GROUP)


def codes_of(got_ref, block, g):
    return got_ref[block, group_rows(g), :].astype(jnp.int32)


def add_norms(got_ref, norm_ref, block, g, total):
    part = group_rows(g)
    code = codes_of(got_ref, block, g)
    rest = code & 127
    low, high = norm_ref[part, :LANES], norm_ref[part, LANES:]
    return total + jnp.where(code < LANES, lane_gather(low, rest), lane_gather(high, rest))


def scale_of(total):
    norm = jnp.sum(total, axis=0, keepdims=True)
    return jnp.broadcast_to(lax.rsqrt(norm + norm_epsilon), (GROUP, LANES))


def decode_part(got_ref, table_ref, block, g, scale, ut_ref, lanes):
    code = codes_of(got_ref, block, g).astype(jnp.int16)
    rest = code & 127
    is_low = code < LANES
    for i in range(SUB):
        low, high = table_ref[g, i, :, :LANES], table_ref[g, i, :, LANES:]
        value = jnp.where(is_low, lane_gather(low, rest), lane_gather(high, rest))
        rows = group_rows(g * SUB + i)
        ut_ref[rows, lanes] = (value.astype(jnp.float32) * scale).astype(jnp.bfloat16)


def block_lanes(j):
    return slice(j * LANES, (j + 1) * LANES)


def key_row(got_ref, j, line):
    return got_ref[j, SUBQ : SUBQ + 16, :].astype(jnp.float32)[line : line + 1, :]


def spread_keys(got_ref, line, keys_ref):
    for j in range(SHARDS):
        key = key_row(got_ref, j, line)
        keys_ref[j * LANES : (j + 1) * LANES, :] = jnp.broadcast_to(key, (LANES, LANES)).T


def key_line(got_ref, j, line):
    key = key_row(got_ref, j, line)
    return jnp.broadcast_to(jnp.where(key == 0.0, -1.0, key), (8, LANES))


def tiles(x):
    return x.reshape(x.shape[0] // 8, 8, LANES)


def fold_lanes(row_best):
    return jnp.max(row_best.T, axis=0, keepdims=True)


def parts_of(rows):
    half = RECV // 2
    return [slice(r, min(r + half, rows)) for r in range(0, rows, half)]


def scales(got_ref, norm_ref, n):
    totals = [jnp.zeros((GROUP, LANES), jnp.float32)] * PER
    for g in range(GROUPS):
        totals = [add_norms(got_ref, norm_ref, n * PER + h, g, totals[h]) for h in range(PER)]
    return [scale_of(t) for t in totals]


def chunk_scores(n, parts, u_ref, ut, keys_ref, line_of, best_ref, old_ref, own, between):
    cols = [jnp.full((8, LANES), -1.0, jnp.float32)] * PER
    for q, rows in enumerate(parts):
        scores = jnp.dot(u_ref[rows, :], ut[...], preferred_element_type=jnp.float32)
        between(q)
        key = tiles(keys_ref[rows, :])
        best = None if old_ref is None else tiles(old_ref[rows, :])
        for h in range(PER):
            part = tiles(scores[:, h * LANES : (h + 1) * LANES])
            ok = key == line_of(h)[None]
            if own and rows.stop > n * SIDE:
                row = iota(part.shape, 0) * 8 + iota(part.shape, 1)
                ok = ok & (row != iota(part.shape, 2) + (h * LANES + n * SIDE - rows.start))
            part = jnp.where(ok, part, -1.0)
            best = part if best is None else jnp.maximum(best, part)
            cols[h] = jnp.maximum(cols[h], jnp.max(part, axis=0))
        best_ref[rows, :] = best.reshape(rows.stop - rows.start, LANES)
    return [jnp.max(c, axis=0, keepdims=True) for c in cols]


def own_piece(n, got_ref, u_ref, ut_ref, keys_ref, best_ref, out_ref, between, alone=False):
    cols = chunk_scores(
        n,
        parts_of((n + 1) * SIDE),
        u_ref,
        ut_ref.at[:, n * SIDE : (n + 1) * SIDE],
        keys_ref,
        lambda h: key_line(got_ref, n * PER + h, 0),
        best_ref,
        None if alone else best_ref,
        True,
        between,
    )
    for h in range(PER):
        j = h if alone else n * PER + h
        out_ref[j : j + 1, :] = cols[h]


def own_kernel(
    got_ref, table_ref, norm_ref, ut_ref, u_ref, slots_ref, pairs_ref, best_ref, out_ref
):
    eye = (iota((SIDE, SIDE), 0) == iota((SIDE, SIDE), 1)).astype(jnp.bfloat16)

    def decode_chunk(n, groups, scale):
        for g in groups:
            for h in range(PER):
                j = n * PER + h
                decode_part(got_ref, table_ref, j, g, scale[h], ut_ref, block_lanes(j))

    def turn_chunk(n):
        lanes = slice(n * SIDE, (n + 1) * SIDE)
        u_ref[lanes, :] = lax.dot_general(
            eye, ut_ref[:, lanes], (((1,), (1,)), ((), ())), preferred_element_type=jnp.float32
        ).astype(jnp.bfloat16)

    spread_keys(got_ref, 0, slots_ref)
    spread_keys(got_ref, 1, pairs_ref)
    best_ref[...] = jnp.full(best_ref.shape, -1.0, jnp.float32)
    out_ref[...] = jnp.full(out_ref.shape, -1.0, jnp.float32)
    decode_chunk(0, range(GROUPS), scales(got_ref, norm_ref, 0))
    turn_chunk(0)
    for n in range(1, CHUNKS + 1):
        if n < CHUNKS:
            scale = scales(got_ref, norm_ref, n)
            if n - 1 >= EARLY:
                decode_chunk(n, range(GROUPS), scale)
        if n - 1 < EARLY:
            count = len(parts_of(n * SIDE))

            def between(q):
                if n < CHUNKS:
                    decode_chunk(n, range(q * GROUPS // count, (q + 1) * GROUPS // count), scale)

            own_piece(n - 1, got_ref, u_ref, ut_ref, slots_ref, best_ref, out_ref, between)
        if n < CHUNKS:
            turn_chunk(n)


def fold_rows(best_ref, out_ref, rows, join):
    for j in range(rows.start // LANES, rows.stop // LANES):
        row = fold_lanes(best_ref[j * LANES : (j + 1) * LANES, :])
        if join:
            row = jnp.maximum(out_ref[j : j + 1, :], row)
        out_ref[j : j + 1, :] = row


def within_kernel(
    got_ref, ut_ref, u_ref, slots_ref, best_in, early_in, best_more, more_in, crossed_ref,
    out_ref, row_ref, best_ref,
):
    out_ref[...] = early_in[...]
    out_ref[EARLY * PER : (EARLY + 1) * PER, :] = more_in[...]
    rows = (EARLY + 1) * SIDE
    best_ref[:rows, :] = jnp.maximum(best_in[:rows, :], best_more[...])
    best_ref[rows:, :] = best_in[rows:, :]
    parts = parts_of(RECV)

    def between(n, q):
        if n == FOLD:
            fold_rows(crossed_ref, row_ref, parts[q], False)
        if n == CHUNKS - 1 and q > 0:
            fold_rows(best_ref, out_ref, parts[q - 1], True)

    for n in range(EARLY + 1, CHUNKS):
        own_piece(
            n, got_ref, u_ref, ut_ref, slots_ref, best_ref, out_ref, lambda q: between(n, q)
        )
    fold_rows(best_ref, out_ref, parts[-1], True)


def decode_left(left_ref, table_ref, j, groups, scale, ut):
    for g in groups:
        for h in range(PER):
            decode_part(left_ref, table_ref, j + h, g, scale[h], ut, block_lanes(h))


def share(groups, q, count):
    return range(q * groups // count, (q + 1) * groups // count)


def left_scores(left_ref, j, pairs_ref, u_ref, ut, best_ref, old_ref, out_ref, row, between):
    cols = chunk_scores(
        0,
        parts_of(RECV),
        u_ref,
        ut,
        pairs_ref,
        lambda h: key_line(left_ref, j + h, 0),
        best_ref,
        old_ref,
        False,
        between,
    )
    for h in range(PER):
        out_ref[row + h : row + h + 1, :] = cols[h]


def first_kernel(
    pairs_ref, left_ref, table_ref, norm_ref, u_ref, got_ref, own_ref, slots_ref,
    out_ref, best_ref, ut_b, best_more, more_ref, ut_a,
):
    uts = (ut_a, ut_b)
    scale = scales(left_ref, norm_ref, 0)
    count = len(parts_of((EARLY + 1) * SIDE))
    own_piece(
        EARLY,
        got_ref,
        u_ref,
        own_ref,
        slots_ref,
        best_more,
        more_ref,
        lambda q: decode_left(left_ref, table_ref, 0, share(GROUPS, q, count), scale, ut_a),
        True,
    )
    for n in range(HALF // PER - 1):
        j = (n + 1) * PER
        scale = scales(left_ref, norm_ref, n + 1)
        left_scores(
            left_ref,
            n * PER,
            pairs_ref,
            u_ref,
            uts[n % 2],
            best_ref,
            best_ref if n else None,
            out_ref,
            n * PER,
            lambda q: decode_left(
                left_ref, table_ref, j, share(GROUPS, q, 2), scale, uts[(n + 1) % 2]
            ),
        )


def second_kernel(
    pairs_ref, before_ref, left_ref, table_ref, norm_ref, u_ref, best_in, ut_in,
    out_ref, best_ref, ut_a, ut_b,
):
    uts = (ut_in, ut_a, ut_b)
    chunks = HALF // PER
    for n in range(chunks + 1):
        now = uts[0] if n == 0 else uts[1 + (n - 1) % 2]
        scale = scales(left_ref, norm_ref, n) if n < chunks else None

        def between(q):
            if n < chunks:
                decode_left(
                    left_ref, table_ref, n * PER, share(GROUPS, q, 2), scale, uts[1 + n % 2]
                )

        left_scores(
            left_ref if n else before_ref,
            (n - 1) * PER if n else HALF - PER,
            pairs_ref,
            u_ref,
            now,
            best_ref,
            best_ref if n else best_in,
            out_ref,
            n * PER,
            between,
        )


def pick_kernel(got_ref, dest_ref, rank_ref, within_ref, near_ref):
    dest, rank = dest_ref[...], rank_ref[...]
    within = jnp.zeros((8, LANES), jnp.float32)
    near = within
    for o in range(SHARDS):
        here = dest == o
        first = jnp.broadcast_to(got_ref[o, 0:1, :], (8, LANES))
        second = jnp.broadcast_to(got_ref[o, 1:2, :], (8, LANES))
        within = jnp.where(here, lane_gather(first, rank), within)
        near = jnp.where(here, lane_gather(second, rank), near)
    within_ref[...] = within
    near_ref[...] = near


def kernel_call(body, shapes, count, scratch=(), name=None, flops=0):
    return pl.pallas_call(
        body,
        out_shape=shapes,
        in_specs=[VMEM] * count,
        out_specs=[VMEM] * len(shapes),
        scratch_shapes=list(scratch),
        compiler_params=pltpu.CompilerParams(vmem_limit_bytes=16 << 20),
        name=name,
        cost_estimate=pl.CostEstimate(flops=flops, bytes_accessed=1 << 20, transcendentals=0),
    )


def shape(dims, kind):
    return jax.ShapeDtypeStruct(dims, kind)


bf16, f32, i32 = jnp.bfloat16, jnp.float32, jnp.int32
K_OWN = (
    own_kernel,
    [
        shape((EMB, RECV), bf16),
        shape((RECV, EMB), bf16),
        shape((RECV, LANES), f32),
        shape((RECV, LANES), f32),
        shape((RECV, LANES), f32),
        shape((SHARDS, LANES), f32),
    ],
    3,
)
UT = pltpu.VMEM((EMB, SIDE), bf16)
BEST = pltpu.VMEM((RECV, LANES), f32)
HALF = SHARDS // 2
K_FIRST = (
    first_kernel,
    [
        shape((HALF - PER, LANES), f32),
        shape((RECV, LANES), f32),
        shape((EMB, SIDE), bf16),
        shape(((EARLY + 1) * SIDE, LANES), f32),
        shape((PER, LANES), f32),
    ],
    8,
    [UT],
)
K_SECOND = (
    second_kernel,
    [shape((HALF + PER, LANES), f32), shape((RECV, LANES), f32)],
    8,
    [UT, UT],
)
K_WITHIN = (
    within_kernel, [shape((SHARDS, LANES), f32), shape((SHARDS, LANES), f32)], 9, [BEST]
)
K_PICK = (pick_kernel, [shape((8, LANES), f32), shape((8, LANES), f32)], 3)


def route_call(*operands):
    small = pltpu.VMEM((8, LANES), i32)
    outside = pl.BlockSpec(memory_space=pltpu.HBM)
    return pl.pallas_call(
        route_kernel,
        out_shape=[
            shape((SHARDS, BLOCK, LANES), bf16),
            shape((8, LANES), i32),
            shape((8, LANES), i32),
        ],
        in_specs=[outside] * 4,
        out_specs=[outside, VMEM, VMEM],
        scratch_shapes=[
            pltpu.VMEM((SHARDS * 64, LANES), i32),
            small,
            small,
            small,
            pltpu.VMEM((SHARDS, BLOCK, LANES), bf16),
            pltpu.SemaphoreType.DMA((4,)),
            pltpu.SemaphoreType.DMA((SHARDS // OWNERS,)),
        ],
        compiler_params=pltpu.CompilerParams(vmem_limit_bytes=16 << 20),
        name="route",
    )(*[pltpu.with_memory_space_constraint(x, pltpu.HBM) for x in operands])


def from_behind(x, axis, by):
    peers = lax.axis_size(axis)
    return lax.ppermute(x, axis, [(i, (i + by) % peers) for i in range(peers)])


def tables_of(codebook):
    turned = jnp.swapaxes(codebook, 1, 2)
    wide = turned.astype(f32)
    norms = jnp.sum(wide * wide, axis=1)
    return turned.reshape(GROUPS, GROUP, SUB, CODES_K).transpose(0, 2, 1, 3), norms


def scores_of(got, left, table, norms):
    ut, u, slots, pairs, best, early = kernel_call(*K_OWN, name="own", flops=8 << 30)(
        got, table, norms
    )
    cols_a, partial, ut_last, best_more, more = kernel_call(
        *K_FIRST, name="first", flops=8 << 30
    )(pairs, left[0], table, norms, u, got, ut, slots)
    cols_b, crossed = kernel_call(*K_SECOND, name="second", flops=8 << 30)(
        pairs, left[0], left[1], table, norms, u, partial, ut_last
    )

    def within():
        return kernel_call(*K_WITHIN, name="within", flops=4 << 30)(
            got, ut, u, slots, best, early, best_more, more, crossed
        )

    return within, jnp.concatenate([cols_a, cols_b], axis=0)


def on_device(codes, cluster_ids, cluster_owner, left_pair, codebook):
    send, dest, rank = route_call(
        codes,
        cluster_ids.reshape(8, LANES),
        cluster_owner.reshape(8, LANES),
        left_pair.reshape(8, LANES),
    )
    table, norms = tables_of(codebook)
    got = lax.all_to_all(send, "shard", split_axis=0, concat_axis=0, tiled=True)
    left = [from_behind(got[h * HALF : (h + 1) * HALF], "blk", 1) for h in range(2)]
    within, for_left = scores_of(got, left, table, norms)
    from_right = from_behind(for_left, "blk", -1)
    within, from_left = within()
    near = jnp.maximum(from_left, from_right)
    answers = jnp.stack([within, near], axis=1)
    back = lax.all_to_all(answers, "shard", split_axis=0, concat_axis=0, tiled=True)
    within_max, near_max = kernel_call(*K_PICK, name="pick")(back, dest, rank)
    return within_max.reshape(-1), near_max.reshape(-1)


def solution(mesh):
    in_specs = (P(("shard", "blk"), None), P(("shard", "blk")), P(), P(), P())
    out_specs = (P(("shard", "blk")), P(("shard", "blk")))
    return jax.shard_map(
        on_device, mesh=mesh, in_specs=in_specs, out_specs=out_specs, check_vma=False
    )
```

```python
import functools

import jax
import jax.numpy as jnp
from jax import lax
from jax.experimental import pallas as pl
from jax.experimental.pallas import tpu as pltpu
from jax.sharding import PartitionSpec as P

EMB = 1024
SUBQ = 128
SUB = 8
CODES_K = 256
CPD = 8
LANES = 128
SHARDS = 16
CAP = 128
RECV = SHARDS * CAP
BLOCK = SUBQ + 16
norm_epsilon = 1e-06

VMEM = pl.BlockSpec(memory_space=pltpu.VMEM)


def lane_gather(table, index):
    numbers = lax.GatherDimensionNumbers(
        offset_dims=(),
        collapsed_slice_dims=(1,),
        start_index_map=(1,),
        operand_batching_dims=(0,),
        start_indices_batching_dims=(0,),
    )
    return lax.gather(
        table,
        index[..., None],
        numbers,
        slice_sizes=(1, 1),
        mode=lax.GatherScatterMode.PROMISE_IN_BOUNDS,
    )


def iota(shape, axis):
    return lax.broadcasted_iota(jnp.int32, shape, axis)


def route_kernel(
    codes_hbm, ids_hbm, owner_hbm, pair_hbm, send_hbm, dest_ref, rank_ref,
    codes_ref, ids_ref, owner_ref, pair_ref, send_ref, in_sem, out_sem,
):
    loads = [
        pltpu.make_async_copy(src, dst, in_sem.at[k])
        for k, (src, dst) in enumerate(
            [
                (owner_hbm, owner_ref),
                (ids_hbm, ids_ref),
                (pair_hbm, pair_ref),
                (codes_hbm, codes_ref),
            ]
        )
    ]
    for load in loads:
        load.start()
    column = lax.axis_index("blk")
    full = (8, LANES)
    sub, lane = iota((LANES, LANES), 0), iota((LANES, LANES), 1)
    loads[0].wait()
    loads[1].wait()
    owner_row = owner_ref[pl.ds(column, 1), :]
    local = ids_ref[...] - column * LANES
    dest = lane_gather(jnp.broadcast_to(owner_row, full), local)
    member = jnp.concatenate([(dest == o).astype(jnp.float32) for o in range(SHARDS)], axis=0)
    member = member.astype(jnp.bfloat16)
    before = (sub < lane).astype(jnp.bfloat16)
    in_row = jnp.dot(member, before, preferred_element_type=jnp.float32)
    above = ((sub // 8 == lane // 8) & (lane < sub)).astype(jnp.bfloat16)
    rows_above = jnp.dot(above, member, preferred_element_type=jnp.float32)
    count = in_row + jnp.sum(rows_above, axis=1, keepdims=True)
    rank = jnp.zeros(full, jnp.float32)
    for o in range(SHARDS):
        rank = jnp.where(dest == o, count[o * 8 : (o + 1) * 8, :], rank)
    rank = rank.astype(jnp.int32)
    dest_ref[...] = dest
    rank_ref[...] = rank
    owner_sq = jnp.broadcast_to(owner_row, (LANES, LANES))
    same = (owner_sq.T == owner_sq) & (sub < lane)
    slot_row = jnp.sum(same.astype(jnp.int32), axis=0, keepdims=True)
    slot = lane_gather(jnp.broadcast_to(slot_row, full), local)
    loads[2].wait()
    pair_row = pair_ref[pl.ds(column, 1), :]
    pair = lane_gather(jnp.broadcast_to(pair_row, full), local)
    slot_f = (slot + 1).astype(jnp.float32)
    pair_f = (pair + 1).astype(jnp.float32)
    slot_line = jnp.concatenate([slot_f[k : k + 1, :] for k in range(8)], axis=1)
    pair_line = jnp.concatenate([pair_f[k : k + 1, :] for k in range(8)], axis=1)
    tail_row = iota((16, 1024), 0)
    tail = jnp.where(tail_row == 0, slot_line, jnp.where(tail_row == 1, pair_line, 0.0))
    loads[3].wait()
    codes_t = codes_ref[...].astype(jnp.float32).T
    left = jnp.concatenate([codes_t, tail], axis=0).astype(jnp.bfloat16)
    stores = []
    for o in range(0, SHARDS, OWNERS):
        picks = []
        for p in range(OWNERS):
            key = jnp.where(dest == o + p, rank, -1)
            pick = [
                (jnp.broadcast_to(key[k : k + 1, :], (LANES, LANES)) == sub).astype(jnp.float32)
                for k in range(8)
            ]
            picks.append(jnp.concatenate(pick, axis=1))
        pick = jnp.concatenate(picks, axis=0).astype(jnp.bfloat16)
        block = lax.dot_general(
            left, pick, (((1,), (1,)), ((), ())), preferred_element_type=jnp.float32
        ).astype(jnp.bfloat16)
        for p in range(OWNERS):
            send_ref[o + p] = block[:, p * LANES : (p + 1) * LANES]
        part = pl.ds(o, OWNERS)
        store = pltpu.make_async_copy(
            send_ref.at[part], send_hbm.at[part], out_sem.at[o // OWNERS]
        )
        store.start()
        stores.append(store)
    for store in stores:
        store.wait()


OWNERS = 2


FOLD = 6
EARLY = 5
SIDE = 256
PER = SIDE // CAP
CHUNKS = RECV // SIDE
GROUP = 16
GROUPS = SUBQ // GROUP


def group_rows(g):
    if isinstance(g, int):
        return slice(g * GROUP, (g + 1) * GROUP)
    return pl.ds(pl.multiple_of(g * GROUP, GROUP), GROUP)


def codes_of(got_ref, block, g):
    return got_ref[block, group_rows(g), :].astype(jnp.int32)


def add_norms(got_ref, norm_ref, block, g, total):
    part = group_rows(g)
    code = codes_of(got_ref, block, g)
    rest = code & 127
    low, high = norm_ref[part, :LANES], norm_ref[part, LANES:]
    return total + jnp.where(code < LANES, lane_gather(low, rest), lane_gather(high, rest))


def scale_of(total):
    norm = jnp.sum(total, axis=0, keepdims=True)
    return jnp.broadcast_to(lax.rsqrt(norm + norm_epsilon), (GROUP, LANES))


def decode_part(got_ref, table_ref, block, g, scale, ut_ref, lanes):
    code = codes_of(got_ref, block, g).astype(jnp.int16)
    rest = code & 127
    is_low = code < LANES
    for i in range(SUB):
        low, high = table_ref[g, i, :, :LANES], table_ref[g, i, :, LANES:]
        value = jnp.where(is_low, lane_gather(low, rest), lane_gather(high, rest))
        rows = group_rows(g * SUB + i)
        ut_ref[rows, lanes] = (value.astype(jnp.float32) * scale).astype(jnp.bfloat16)


def block_lanes(j):
    return slice(j * LANES, (j + 1) * LANES)


def key_row(got_ref, j, line):
    return got_ref[j, SUBQ : SUBQ + 16, :].astype(jnp.float32)[line : line + 1, :]


def spread_keys(got_ref, line, keys_ref):
    for j in range(SHARDS):
        key = key_row(got_ref, j, line)
        keys_ref[j * LANES : (j + 1) * LANES, :] = jnp.broadcast_to(key, (LANES, LANES)).T


def key_line(got_ref, j, line):
    key = key_row(got_ref, j, line)
    return jnp.broadcast_to(jnp.where(key == 0.0, -1.0, key), (8, LANES))


def tiles(x):
    return x.reshape(x.shape[0] // 8, 8, LANES)


def fold_lanes(row_best):
    return jnp.max(row_best.T, axis=0, keepdims=True)


def parts_of(rows):
    half = RECV // 2
    return [slice(r, min(r + half, rows)) for r in range(0, rows, half)]


def scales(got_ref, norm_ref, n):
    totals = [jnp.zeros((GROUP, LANES), jnp.float32)] * PER
    for g in range(GROUPS):
        totals = [add_norms(got_ref, norm_ref, n * PER + h, g, totals[h]) for h in range(PER)]
    return [scale_of(t) for t in totals]


def chunk_scores(n, parts, u_ref, ut, keys_ref, line_of, best_ref, old_ref, own, between):
    cols = [jnp.full((8, LANES), -1.0, jnp.float32)] * PER
    for q, rows in enumerate(parts):
        scores = jnp.dot(u_ref[rows, :], ut[...], preferred_element_type=jnp.float32)
        between(q)
        key = tiles(keys_ref[rows, :])
        best = None if old_ref is None else tiles(old_ref[rows, :])
        for h in range(PER):
            part = tiles(scores[:, h * LANES : (h + 1) * LANES])
            ok = key == line_of(h)[None]
            if own and rows.stop > n * SIDE:
                row = iota(part.shape, 0) * 8 + iota(part.shape, 1)
                ok = ok & (row != iota(part.shape, 2) + (h * LANES + n * SIDE - rows.start))
            part = jnp.where(ok, part, -1.0)
            best = part if best is None else jnp.maximum(best, part)
            cols[h] = jnp.maximum(cols[h], jnp.max(part, axis=0))
        best_ref[rows, :] = best.reshape(rows.stop - rows.start, LANES)
    return [jnp.max(c, axis=0, keepdims=True) for c in cols]


def own_piece(n, got_ref, u_ref, ut_ref, keys_ref, best_ref, out_ref, between, alone=False):
    cols = chunk_scores(
        n,
        parts_of((n + 1) * SIDE),
        u_ref,
        ut_ref.at[:, n * SIDE : (n + 1) * SIDE],
        keys_ref,
        lambda h: key_line(got_ref, n * PER + h, 0),
        best_ref,
        None if alone else best_ref,
        True,
        between,
    )
    for h in range(PER):
        j = h if alone else n * PER + h
        out_ref[j : j + 1, :] = cols[h]


def own_kernel(
    got_ref, table_ref, norm_ref, ut_ref, u_ref, slots_ref, pairs_ref, best_ref, out_ref
):
    eye = (iota((SIDE, SIDE), 0) == iota((SIDE, SIDE), 1)).astype(jnp.bfloat16)

    def decode_chunk(n, groups, scale):
        for g in groups:
            for h in range(PER):
                j = n * PER + h
                decode_part(got_ref, table_ref, j, g, scale[h], ut_ref, block_lanes(j))

    def turn_chunk(n):
        lanes = slice(n * SIDE, (n + 1) * SIDE)
        u_ref[lanes, :] = lax.dot_general(
            eye, ut_ref[:, lanes], (((1,), (1,)), ((), ())), preferred_element_type=jnp.float32
        ).astype(jnp.bfloat16)

    spread_keys(got_ref, 0, slots_ref)
    spread_keys(got_ref, 1, pairs_ref)
    best_ref[...] = jnp.full(best_ref.shape, -1.0, jnp.float32)
    out_ref[...] = jnp.full(out_ref.shape, -1.0, jnp.float32)
    decode_chunk(0, range(GROUPS), scales(got_ref, norm_ref, 0))
    turn_chunk(0)
    for n in range(1, CHUNKS + 1):
        if n < CHUNKS:
            scale = scales(got_ref, norm_ref, n)
            if n - 1 >= EARLY:
                decode_chunk(n, range(GROUPS), scale)
        if n - 1 < EARLY:
            count = len(parts_of(n * SIDE))

            def between(q):
                if n < CHUNKS:
                    decode_chunk(n, range(q * GROUPS // count, (q + 1) * GROUPS // count), scale)

            own_piece(n - 1, got_ref, u_ref, ut_ref, slots_ref, best_ref, out_ref, between)
        if n < CHUNKS:
            turn_chunk(n)


def fold_rows(best_ref, out_ref, rows, join):
    for j in range(rows.start // LANES, rows.stop // LANES):
        row = fold_lanes(best_ref[j * LANES : (j + 1) * LANES, :])
        if join:
            row = jnp.maximum(out_ref[j : j + 1, :], row)
        out_ref[j : j + 1, :] = row


def within_kernel(
    got_ref, ut_ref, u_ref, slots_ref, best_in, early_in, best_more, more_in, crossed_ref,
    out_ref, row_ref, best_ref,
):
    out_ref[...] = early_in[...]
    out_ref[EARLY * PER : (EARLY + 1) * PER, :] = more_in[...]
    rows = (EARLY + 1) * SIDE
    best_ref[:rows, :] = jnp.maximum(best_in[:rows, :], best_more[...])
    best_ref[rows:, :] = best_in[rows:, :]
    parts = parts_of(RECV)

    def between(n, q):
        if n == FOLD:
            fold_rows(crossed_ref, row_ref, parts[q], False)
        if n == CHUNKS - 1 and q > 0:
            fold_rows(best_ref, out_ref, parts[q - 1], True)

    for n in range(EARLY + 1, CHUNKS):
        own_piece(
            n, got_ref, u_ref, ut_ref, slots_ref, best_ref, out_ref, lambda q: between(n, q)
        )
    fold_rows(best_ref, out_ref, parts[-1], True)


def decode_left(left_ref, table_ref, j, groups, scale, ut):
    for g in groups:
        for h in range(PER):
            decode_part(left_ref, table_ref, j + h, g, scale[h], ut, block_lanes(h))


def share(groups, q, count):
    return range(q * groups // count, (q + 1) * groups // count)


def left_scores(left_ref, j, pairs_ref, u_ref, ut, best_ref, old_ref, out_ref, row, between):
    cols = chunk_scores(
        0,
        parts_of(RECV),
        u_ref,
        ut,
        pairs_ref,
        lambda h: key_line(left_ref, j + h, 0),
        best_ref,
        old_ref,
        False,
        between,
    )
    for h in range(PER):
        out_ref[row + h : row + h + 1, :] = cols[h]


def first_kernel(
    pairs_ref, left_ref, table_ref, norm_ref, u_ref, got_ref, own_ref, slots_ref,
    out_ref, best_ref, ut_b, best_more, more_ref, ut_a,
):
    uts = (ut_a, ut_b)
    scale = scales(left_ref, norm_ref, 0)
    count = len(parts_of((EARLY + 1) * SIDE))
    own_piece(
        EARLY,
        got_ref,
        u_ref,
        own_ref,
        slots_ref,
        best_more,
        more_ref,
        lambda q: decode_left(left_ref, table_ref, 0, share(GROUPS, q, count), scale, ut_a),
        True,
    )
    for n in range(HALF // PER - 1):
        j = (n + 1) * PER
        scale = scales(left_ref, norm_ref, n + 1)
        left_scores(
            left_ref,
            n * PER,
            pairs_ref,
            u_ref,
            uts[n % 2],
            best_ref,
            best_ref if n else None,
            out_ref,
            n * PER,
            lambda q: decode_left(
                left_ref, table_ref, j, share(GROUPS, q, 2), scale, uts[(n + 1) % 2]
            ),
        )


def second_kernel(
    pairs_ref, before_ref, left_ref, table_ref, norm_ref, u_ref, best_in, ut_in,
    out_ref, best_ref, ut_a, ut_b,
):
    uts = (ut_in, ut_a, ut_b)
    chunks = HALF // PER
    for n in range(chunks + 1):
        now = uts[0] if n == 0 else uts[1 + (n - 1) % 2]
        scale = scales(left_ref, norm_ref, n) if n < chunks else None

        def between(q):
            if n < chunks:
                decode_left(
                    left_ref, table_ref, n * PER, share(GROUPS, q, 2), scale, uts[1 + n % 2]
                )

        left_scores(
            left_ref if n else before_ref,
            (n - 1) * PER if n else HALF - PER,
            pairs_ref,
            u_ref,
            now,
            best_ref,
            best_ref if n else best_in,
            out_ref,
            n * PER,
            between,
        )


def pick_kernel(got_ref, dest_ref, rank_ref, within_ref, near_ref):
    dest, rank = dest_ref[...], rank_ref[...]
    within = jnp.zeros((8, LANES), jnp.float32)
    near = within
    for o in range(SHARDS):
        here = dest == o
        first = jnp.broadcast_to(got_ref[o, 0:1, :], (8, LANES))
        second = jnp.broadcast_to(got_ref[o, 1:2, :], (8, LANES))
        within = jnp.where(here, lane_gather(first, rank), within)
        near = jnp.where(here, lane_gather(second, rank), near)
    within_ref[...] = within
    near_ref[...] = near


def kernel_call(body, shapes, count, scratch=(), name=None, flops=0):
    return pl.pallas_call(
        body,
        out_shape=shapes,
        in_specs=[VMEM] * count,
        out_specs=[VMEM] * len(shapes),
        scratch_shapes=list(scratch),
        compiler_params=pltpu.CompilerParams(vmem_limit_bytes=16 << 20),
        name=name,
        cost_estimate=pl.CostEstimate(flops=flops, bytes_accessed=1 << 20, transcendentals=0),
    )


def shape(dims, kind):
    return jax.ShapeDtypeStruct(dims, kind)


bf16, f32, i32 = jnp.bfloat16, jnp.float32, jnp.int32
K_OWN = (
    own_kernel,
    [
        shape((EMB, RECV), bf16),
        shape((RECV, EMB), bf16),
        shape((RECV, LANES), f32),
        shape((RECV, LANES), f32),
        shape((RECV, LANES), f32),
        shape((SHARDS, LANES), f32),
    ],
    3,
)
UT = pltpu.VMEM((EMB, SIDE), bf16)
BEST = pltpu.VMEM((RECV, LANES), f32)
HALF = SHARDS // 2
K_FIRST = (
    first_kernel,
    [
        shape((HALF - PER, LANES), f32),
        shape((RECV, LANES), f32),
        shape((EMB, SIDE), bf16),
        shape(((EARLY + 1) * SIDE, LANES), f32),
        shape((PER, LANES), f32),
    ],
    8,
    [UT],
)
K_SECOND = (
    second_kernel,
    [shape((HALF + PER, LANES), f32), shape((RECV, LANES), f32)],
    8,
    [UT, UT],
)
K_WITHIN = (
    within_kernel, [shape((SHARDS, LANES), f32), shape((SHARDS, LANES), f32)], 9, [BEST]
)
K_PICK = (pick_kernel, [shape((8, LANES), f32), shape((8, LANES), f32)], 3)


def route_call(*operands):
    small = pltpu.VMEM((8, LANES), i32)
    outside = pl.BlockSpec(memory_space=pltpu.HBM)
    return pl.pallas_call(
        route_kernel,
        out_shape=[
            shape((SHARDS, BLOCK, LANES), bf16),
            shape((8, LANES), i32),
            shape((8, LANES), i32),
        ],
        in_specs=[outside] * 4,
        out_specs=[outside, VMEM, VMEM],
        scratch_shapes=[
            pltpu.VMEM((SHARDS * 64, LANES), i32),
            small,
            small,
            small,
            pltpu.VMEM((SHARDS, BLOCK, LANES), bf16),
            pltpu.SemaphoreType.DMA((4,)),
            pltpu.SemaphoreType.DMA((SHARDS // OWNERS,)),
        ],
        compiler_params=pltpu.CompilerParams(vmem_limit_bytes=16 << 20),
        name="route",
    )(*[pltpu.with_memory_space_constraint(x, pltpu.HBM) for x in operands])


def from_behind(x, axis, by):
    peers = lax.axis_size(axis)
    return lax.ppermute(x, axis, [(i, (i + by) % peers) for i in range(peers)])


def tables_of(codebook):
    turned = jnp.swapaxes(codebook, 1, 2)
    wide = turned.astype(f32)
    norms = jnp.sum(wide * wide, axis=1)
    return turned.reshape(GROUPS, GROUP, SUB, CODES_K).transpose(0, 2, 1, 3), norms


def scores_of(got, left, table, norms):
    ut, u, slots, pairs, best, early = kernel_call(*K_OWN, name="own", flops=2 << 30)(
        got, table, norms
    )
    cols_a, partial, ut_last, best_more, more = kernel_call(
        *K_FIRST, name="first", flops=8 << 30
    )(pairs, left[0], table, norms, u, got, ut, slots)
    cols_b, crossed = kernel_call(*K_SECOND, name="second", flops=8 << 30)(
        pairs, left[0], left[1], table, norms, u, partial, ut_last
    )

    def within():
        return kernel_call(*K_WITHIN, name="within", flops=4 << 30)(
            got, ut, u, slots, best, early, best_more, more, crossed
        )

    return within, jnp.concatenate([cols_a, cols_b], axis=0)


def on_device(codes, cluster_ids, cluster_owner, left_pair, codebook):
    send, dest, rank = route_call(
        codes,
        cluster_ids.reshape(8, LANES),
        cluster_owner.reshape(8, LANES),
        left_pair.reshape(8, LANES),
    )
    table, norms = tables_of(codebook)
    got = lax.all_to_all(send, "shard", split_axis=0, concat_axis=0, tiled=True)
    left = [from_behind(got[h * HALF : (h + 1) * HALF], "blk", 1) for h in range(2)]
    within, for_left = scores_of(got, left, table, norms)
    from_right = from_behind(for_left, "blk", -1)
    within, from_left = within()
    near = jnp.maximum(from_left, from_right)
    answers = jnp.stack([within, near], axis=1)
    back = lax.all_to_all(answers, "shard", split_axis=0, concat_axis=0, tiled=True)
    within_max, near_max = kernel_call(*K_PICK, name="pick")(back, dest, rank)
    return within_max.reshape(-1), near_max.reshape(-1)


def solution(mesh):
    in_specs = (P(("shard", "blk"), None), P(("shard", "blk")), P(), P(), P())
    out_specs = (P(("shard", "blk")), P(("shard", "blk")))
    return jax.shard_map(
        on_device, mesh=mesh, in_specs=in_specs, out_specs=out_specs, check_vma=False
    )
```

```python
import functools

import jax
import jax.numpy as jnp
from jax import lax
from jax.experimental import pallas as pl
from jax.experimental.pallas import tpu as pltpu
from jax.sharding import PartitionSpec as P

EMB = 1024
SUBQ = 128
SUB = 8
CODES_K = 256
CPD = 8
LANES = 128
SHARDS = 16
CAP = 128
RECV = SHARDS * CAP
BLOCK = SUBQ + 16
norm_epsilon = 1e-06

VMEM = pl.BlockSpec(memory_space=pltpu.VMEM)


def lane_gather(table, index):
    numbers = lax.GatherDimensionNumbers(
        offset_dims=(),
        collapsed_slice_dims=(1,),
        start_index_map=(1,),
        operand_batching_dims=(0,),
        start_indices_batching_dims=(0,),
    )
    return lax.gather(
        table,
        index[..., None],
        numbers,
        slice_sizes=(1, 1),
        mode=lax.GatherScatterMode.PROMISE_IN_BOUNDS,
    )


def iota(shape, axis):
    return lax.broadcasted_iota(jnp.int32, shape, axis)


def route_kernel(
    codes_hbm, ids_hbm, owner_hbm, pair_hbm, send_hbm, dest_ref, rank_ref,
    codes_ref, ids_ref, owner_ref, pair_ref, send_ref, in_sem, out_sem,
):
    loads = [
        pltpu.make_async_copy(src, dst, in_sem.at[k])
        for k, (src, dst) in enumerate(
            [
                (owner_hbm, owner_ref),
                (ids_hbm, ids_ref),
                (pair_hbm, pair_ref),
                (codes_hbm, codes_ref),
            ]
        )
    ]
    for load in loads:
        load.start()
    column = lax.axis_index("blk")
    full = (8, LANES)
    sub, lane = iota((LANES, LANES), 0), iota((LANES, LANES), 1)
    loads[0].wait()
    loads[1].wait()
    owner_row = owner_ref[pl.ds(column, 1), :]
    local = ids_ref[...] - column * LANES
    dest = lane_gather(jnp.broadcast_to(owner_row, full), local)
    member = jnp.concatenate([(dest == o).astype(jnp.float32) for o in range(SHARDS)], axis=0)
    member = member.astype(jnp.bfloat16)
    before = (sub < lane).astype(jnp.bfloat16)
    in_row = jnp.dot(member, before, preferred_element_type=jnp.float32)
    above = ((sub // 8 == lane // 8) & (lane < sub)).astype(jnp.bfloat16)
    rows_above = jnp.dot(above, member, preferred_element_type=jnp.float32)
    count = in_row + jnp.sum(rows_above, axis=1, keepdims=True)
    rank = jnp.zeros(full, jnp.float32)
    for o in range(SHARDS):
        rank = jnp.where(dest == o, count[o * 8 : (o + 1) * 8, :], rank)
    rank = rank.astype(jnp.int32)
    dest_ref[...] = dest
    rank_ref[...] = rank
    owner_sq = jnp.broadcast_to(owner_row, (LANES, LANES))
    same = (owner_sq.T == owner_sq) & (sub < lane)
    slot_row = jnp.sum(same.astype(jnp.int32), axis=0, keepdims=True)
    slot = lane_gather(jnp.broadcast_to(slot_row, full), local)
    loads[2].wait()
    pair_row = pair_ref[pl.ds(column, 1), :]
    pair = lane_gather(jnp.broadcast_to(pair_row, full), local)
    slot_f = (slot + 1).astype(jnp.float32)
    pair_f = (pair + 1).astype(jnp.float32)
    slot_line = jnp.concatenate([slot_f[k : k + 1, :] for k in range(8)], axis=1)
    pair_line = jnp.concatenate([pair_f[k : k + 1, :] for k in range(8)], axis=1)
    tail_row = iota((16, 1024), 0)
    tail = jnp.where(tail_row == 0, slot_line, jnp.where(tail_row == 1, pair_line, 0.0))
    loads[3].wait()
    codes_t = codes_ref[...].astype(jnp.float32).T
    left = jnp.concatenate([codes_t, tail], axis=0).astype(jnp.bfloat16)
    stores = []
    for o in range(0, SHARDS, OWNERS):
        picks = []
        for p in range(OWNERS):
            key = jnp.where(dest == o + p, rank, -1)
            pick = [
                (jnp.broadcast_to(key[k : k + 1, :], (LANES, LANES)) == sub).astype(jnp.float32)
                for k in range(8)
            ]
            picks.append(jnp.concatenate(pick, axis=1))
        pick = jnp.concatenate(picks, axis=0).astype(jnp.bfloat16)
        block = lax.dot_general(
            left, pick, (((1,), (1,)), ((), ())), preferred_element_type=jnp.float32
        ).astype(jnp.bfloat16)
        for p in range(OWNERS):
            send_ref[o + p] = block[:, p * LANES : (p + 1) * LANES]
        part = pl.ds(o, OWNERS)
        store = pltpu.make_async_copy(
            send_ref.at[part], send_hbm.at[part], out_sem.at[o // OWNERS]
        )
        store.start()
        stores.append(store)
    for store in stores:
        store.wait()


OWNERS = 2


FOLD = 6
EARLY = 5
SIDE = 256
PER = SIDE // CAP
CHUNKS = RECV // SIDE
GROUP = 16
GROUPS = SUBQ // GROUP


def group_rows(g):
    if isinstance(g, int):
        return slice(g * GROUP, (g + 1) * GROUP)
    return pl.ds(pl.multiple_of(g * GROUP, GROUP), GROUP)


def codes_of(got_ref, block, g):
    return got_ref[block, group_rows(g), :].astype(jnp.int32)


def add_norms(got_ref, norm_ref, block, g, total):
    part = group_rows(g)
    code = codes_of(got_ref, block, g)
    rest = code & 127
    low, high = norm_ref[part, :LANES], norm_ref[part, LANES:]
    return total + jnp.where(code < LANES, lane_gather(low, rest), lane_gather(high, rest))


def scale_of(total):
    norm = jnp.sum(total, axis=0, keepdims=True)
    return jnp.broadcast_to(lax.rsqrt(norm + norm_epsilon), (GROUP, LANES))


def decode_part(got_ref, table_ref, block, g, scale, ut_ref, lanes):
    code = codes_of(got_ref, block, g).astype(jnp.int16)
    rest = code & 127
    is_low = code < LANES
    for i in range(SUB):
        low, high = table_ref[g, i, :, :LANES], table_ref[g, i, :, LANES:]
        value = jnp.where(is_low, lane_gather(low, rest), lane_gather(high, rest))
        rows = group_rows(g * SUB + i)
        ut_ref[rows, lanes] = (value.astype(jnp.float32) * scale).astype(jnp.bfloat16)


def block_lanes(j):
    return slice(j * LANES, (j + 1) * LANES)


def key_row(got_ref, j, line):
    return got_ref[j, SUBQ : SUBQ + 16, :].astype(jnp.float32)[line : line + 1, :]


def spread_keys(got_ref, line, keys_ref):
    for j in range(SHARDS):
        key = key_row(got_ref, j, line)
        keys_ref[j * LANES : (j + 1) * LANES, :] = jnp.broadcast_to(key, (LANES, LANES)).T


def key_line(got_ref, j, line):
    key = key_row(got_ref, j, line)
    return jnp.broadcast_to(jnp.where(key == 0.0, -1.0, key), (8, LANES))


def tiles(x):
    return x.reshape(x.shape[0] // 8, 8, LANES)


def fold_lanes(row_best):
    return jnp.max(row_best.T, axis=0, keepdims=True)


def parts_of(rows):
    half = RECV // 2
    return [slice(r, min(r + half, rows)) for r in range(0, rows, half)]


def scales(got_ref, norm_ref, n):
    totals = [jnp.zeros((GROUP, LANES), jnp.float32)] * PER
    for g in range(GROUPS):
        totals = [add_norms(got_ref, norm_ref, n * PER + h, g, totals[h]) for h in range(PER)]
    return [scale_of(t) for t in totals]


def chunk_scores(n, parts, u_ref, ut, keys_ref, line_of, best_ref, old_ref, own, between):
    cols = [jnp.full((8, LANES), -1.0, jnp.float32)] * PER
    for q, rows in enumerate(parts):
        scores = jnp.dot(u_ref[rows, :], ut[...], preferred_element_type=jnp.float32)
        between(q)
        key = tiles(keys_ref[rows, :])
        best = None if old_ref is None else tiles(old_ref[rows, :])
        for h in range(PER):
            part = tiles(scores[:, h * LANES : (h + 1) * LANES])
            ok = key == line_of(h)[None]
            if own and rows.stop > n * SIDE:
                row = iota(part.shape, 0) * 8 + iota(part.shape, 1)
                ok = ok & (row != iota(part.shape, 2) + (h * LANES + n * SIDE - rows.start))
            part = jnp.where(ok, part, -1.0)
            best = part if best is None else jnp.maximum(best, part)
            cols[h] = jnp.maximum(cols[h], jnp.max(part, axis=0))
        best_ref[rows, :] = best.reshape(rows.stop - rows.start, LANES)
    return [jnp.max(c, axis=0, keepdims=True) for c in cols]


def own_piece(n, got_ref, u_ref, ut_ref, keys_ref, best_ref, out_ref, between, alone=False):
    cols = chunk_scores(
        n,
        parts_of((n + 1) * SIDE),
        u_ref,
        ut_ref.at[:, n * SIDE : (n + 1) * SIDE],
        keys_ref,
        lambda h: key_line(got_ref, n * PER + h, 0),
        best_ref,
        None if alone else best_ref,
        True,
        between,
    )
    for h in range(PER):
        j = h if alone else n * PER + h
        out_ref[j : j + 1, :] = cols[h]


def own_kernel(
    got_ref, table_ref, norm_ref, ut_ref, u_ref, slots_ref, pairs_ref, best_ref, out_ref
):
    eye = (iota((SIDE, SIDE), 0) == iota((SIDE, SIDE), 1)).astype(jnp.bfloat16)

    def decode_chunk(n, groups, scale):
        for g in groups:
            for h in range(PER):
                j = n * PER + h
                decode_part(got_ref, table_ref, j, g, scale[h], ut_ref, block_lanes(j))

    def turn_chunk(n):
        lanes = slice(n * SIDE, (n + 1) * SIDE)
        u_ref[lanes, :] = lax.dot_general(
            eye, ut_ref[:, lanes], (((1,), (1,)), ((), ())), preferred_element_type=jnp.float32
        ).astype(jnp.bfloat16)

    spread_keys(got_ref, 0, slots_ref)
    spread_keys(got_ref, 1, pairs_ref)
    best_ref[...] = jnp.full(best_ref.shape, -1.0, jnp.float32)
    out_ref[...] = jnp.full(out_ref.shape, -1.0, jnp.float32)
    decode_chunk(0, range(GROUPS), scales(got_ref, norm_ref, 0))
    turn_chunk(0)
    for n in range(1, CHUNKS + 1):
        if n < CHUNKS:
            scale = scales(got_ref, norm_ref, n)
            if n - 1 >= EARLY:
                decode_chunk(n, range(GROUPS), scale)
        if n - 1 < EARLY:
            count = len(parts_of(n * SIDE))

            def between(q):
                if n < CHUNKS:
                    decode_chunk(n, range(q * GROUPS // count, (q + 1) * GROUPS // count), scale)

            own_piece(n - 1, got_ref, u_ref, ut_ref, slots_ref, best_ref, out_ref, between)
        if n < CHUNKS:
            turn_chunk(n)


def fold_rows(best_ref, out_ref, rows, join):
    for j in range(rows.start // LANES, rows.stop // LANES):
        row = fold_lanes(best_ref[j * LANES : (j + 1) * LANES, :])
        if join:
            row = jnp.maximum(out_ref[j : j + 1, :], row)
        out_ref[j : j + 1, :] = row


def within_kernel(
    got_ref, ut_ref, u_ref, slots_ref, best_in, early_in, best_more, more_in, crossed_ref,
    out_ref, row_ref, best_ref,
):
    out_ref[...] = early_in[...]
    out_ref[EARLY * PER : (EARLY + 1) * PER, :] = more_in[...]
    rows = (EARLY + 1) * SIDE
    best_ref[:rows, :] = jnp.maximum(best_in[:rows, :], best_more[...])
    best_ref[rows:, :] = best_in[rows:, :]
    parts = parts_of(RECV)

    def between(n, q):
        if n == FOLD:
            fold_rows(crossed_ref, row_ref, parts[q], False)
        if n == CHUNKS - 1 and q > 0:
            fold_rows(best_ref, out_ref, parts[q - 1], True)

    for n in range(EARLY + 1, CHUNKS):
        own_piece(
            n, got_ref, u_ref, ut_ref, slots_ref, best_ref, out_ref, lambda q: between(n, q)
        )
    fold_rows(best_ref, out_ref, parts[-1], True)


def decode_left(left_ref, table_ref, j, groups, scale, ut):
    for g in groups:
        for h in range(PER):
            decode_part(left_ref, table_ref, j + h, g, scale[h], ut, block_lanes(h))


def share(groups, q, count):
    return range(q * groups // count, (q + 1) * groups // count)


def left_scores(left_ref, j, pairs_ref, u_ref, ut, best_ref, old_ref, out_ref, row, between):
    cols = chunk_scores(
        0,
        parts_of(RECV),
        u_ref,
        ut,
        pairs_ref,
        lambda h: key_line(left_ref, j + h, 0),
        best_ref,
        old_ref,
        False,
        between,
    )
    for h in range(PER):
        out_ref[row + h : row + h + 1, :] = cols[h]


def first_kernel(
    pairs_ref, left_ref, table_ref, norm_ref, u_ref, got_ref, own_ref, slots_ref,
    out_ref, best_ref, ut_b, best_more, more_ref, ut_a,
):
    uts = (ut_a, ut_b)
    scale = scales(left_ref, norm_ref, 0)
    count = len(parts_of((EARLY + 1) * SIDE))
    own_piece(
        EARLY,
        got_ref,
        u_ref,
        own_ref,
        slots_ref,
        best_more,
        more_ref,
        lambda q: decode_left(left_ref, table_ref, 0, share(GROUPS, q, count), scale, ut_a),
        True,
    )
    for n in range(HALF // PER - 1):
        j = (n + 1) * PER
        scale = scales(left_ref, norm_ref, n + 1)
        left_scores(
            left_ref,
            n * PER,
            pairs_ref,
            u_ref,
            uts[n % 2],
            best_ref,
            best_ref if n else None,
            out_ref,
            n * PER,
            lambda q: decode_left(
                left_ref, table_ref, j, share(GROUPS, q, 2), scale, uts[(n + 1) % 2]
            ),
        )


def second_kernel(
    pairs_ref, before_ref, left_ref, table_ref, norm_ref, u_ref, best_in, ut_in,
    out_ref, best_ref, ut_a, ut_b,
):
    uts = (ut_in, ut_a, ut_b)
    chunks = HALF // PER
    for n in range(chunks + 1):
        now = uts[0] if n == 0 else uts[1 + (n - 1) % 2]
        scale = scales(left_ref, norm_ref, n) if n < chunks else None

        def between(q):
            if n < chunks:
                decode_left(
                    left_ref, table_ref, n * PER, share(GROUPS, q, 2), scale, uts[1 + n % 2]
                )

        left_scores(
            left_ref if n else before_ref,
            (n - 1) * PER if n else HALF - PER,
            pairs_ref,
            u_ref,
            now,
            best_ref,
            best_ref if n else best_in,
            out_ref,
            n * PER,
            between,
        )


def pick_kernel(got_ref, dest_ref, rank_ref, within_ref, near_ref):
    dest, rank = dest_ref[...], rank_ref[...]
    within = jnp.zeros((8, LANES), jnp.float32)
    near = within
    for o in range(SHARDS):
        here = dest == o
        first = jnp.broadcast_to(got_ref[o, 0:1, :], (8, LANES))
        second = jnp.broadcast_to(got_ref[o, 1:2, :], (8, LANES))
        within = jnp.where(here, lane_gather(first, rank), within)
        near = jnp.where(here, lane_gather(second, rank), near)
    within_ref[...] = within
    near_ref[...] = near


def kernel_call(body, shapes, count, scratch=(), name=None, flops=0):
    return pl.pallas_call(
        body,
        out_shape=shapes,
        in_specs=[VMEM] * count,
        out_specs=[VMEM] * len(shapes),
        scratch_shapes=list(scratch),
        compiler_params=pltpu.CompilerParams(vmem_limit_bytes=16 << 20),
        name=name,
        cost_estimate=pl.CostEstimate(flops=flops, bytes_accessed=1 << 20, transcendentals=0),
    )


def shape(dims, kind):
    return jax.ShapeDtypeStruct(dims, kind)


bf16, f32, i32 = jnp.bfloat16, jnp.float32, jnp.int32
K_OWN = (
    own_kernel,
    [
        shape((EMB, RECV), bf16),
        shape((RECV, EMB), bf16),
        shape((RECV, LANES), f32),
        shape((RECV, LANES), f32),
        shape((RECV, LANES), f32),
        shape((SHARDS, LANES), f32),
    ],
    3,
)
UT = pltpu.VMEM((EMB, SIDE), bf16)
BEST = pltpu.VMEM((RECV, LANES), f32)
HALF = SHARDS // 2
K_FIRST = (
    first_kernel,
    [
        shape((HALF - PER, LANES), f32),
        shape((RECV, LANES), f32),
        shape((EMB, SIDE), bf16),
        shape(((EARLY + 1) * SIDE, LANES), f32),
        shape((PER, LANES), f32),
    ],
    8,
    [UT],
)
K_SECOND = (
    second_kernel,
    [shape((HALF + PER, LANES), f32), shape((RECV, LANES), f32)],
    8,
    [UT, UT],
)
K_WITHIN = (
    within_kernel, [shape((SHARDS, LANES), f32), shape((SHARDS, LANES), f32)], 9, [BEST]
)
K_PICK = (pick_kernel, [shape((8, LANES), f32), shape((8, LANES), f32)], 3)


def route_call(*operands):
    small = pltpu.VMEM((8, LANES), i32)
    outside = pl.BlockSpec(memory_space=pltpu.HBM)
    return pl.pallas_call(
        route_kernel,
        out_shape=[
            shape((SHARDS, BLOCK, LANES), bf16),
            shape((8, LANES), i32),
            shape((8, LANES), i32),
        ],
        in_specs=[outside] * 4,
        out_specs=[outside, VMEM, VMEM],
        scratch_shapes=[
            pltpu.VMEM((SHARDS * 64, LANES), i32),
            small,
            small,
            small,
            pltpu.VMEM((SHARDS, BLOCK, LANES), bf16),
            pltpu.SemaphoreType.DMA((4,)),
            pltpu.SemaphoreType.DMA((SHARDS // OWNERS,)),
        ],
        compiler_params=pltpu.CompilerParams(vmem_limit_bytes=16 << 20),
        name="route",
    )(*[pltpu.with_memory_space_constraint(x, pltpu.HBM) for x in operands])


def from_behind(x, axis, by):
    peers = lax.axis_size(axis)
    return lax.ppermute(x, axis, [(i, (i + by) % peers) for i in range(peers)])


def tables_of(codebook):
    turned = jnp.swapaxes(codebook, 1, 2)
    wide = turned.astype(f32)
    norms = jnp.sum(wide * wide, axis=1)
    return turned.reshape(GROUPS, GROUP, SUB, CODES_K).transpose(0, 2, 1, 3), norms


def scores_of(got, left, table, norms):
    ut, u, slots, pairs, best, early = kernel_call(*K_OWN, name="own", flops=2 << 30)(
        got, table, norms
    )
    cols_a, partial, ut_last, best_more, more = kernel_call(
        *K_FIRST, name="first", flops=8 << 30
    )(pairs, left[0], table, norms, u, got, ut, slots)
    cols_b, crossed = kernel_call(*K_SECOND, name="second", flops=8 << 30)(
        pairs, left[0], left[1], table, norms, u, partial, ut_last
    )

    def within():
        return kernel_call(*K_WITHIN, name="within", flops=4 << 30)(
            got, ut, u, slots, best, early, best_more, more, crossed
        )

    return within, jnp.concatenate([cols_a, cols_b], axis=0)


def on_device(codes, cluster_ids, cluster_owner, left_pair, codebook):
    send, dest, rank = route_call(
        codes,
        cluster_ids.reshape(8, LANES),
        cluster_owner.reshape(8, LANES),
        left_pair.reshape(8, LANES),
    )
    table, norms = tables_of(codebook)
    got = lax.all_to_all(send, "shard", split_axis=0, concat_axis=0, tiled=True)
    got, table, norms = lax.optimization_barrier((got, table, norms))
    left = [from_behind(got[h * HALF : (h + 1) * HALF], "blk", 1) for h in range(2)]
    within, for_left = scores_of(got, left, table, norms)
    from_right = from_behind(for_left, "blk", -1)
    within, from_left = within()
    near = jnp.maximum(from_left, from_right)
    answers = jnp.stack([within, near], axis=1)
    back = lax.all_to_all(answers, "shard", split_axis=0, concat_axis=0, tiled=True)
    within_max, near_max = kernel_call(*K_PICK, name="pick")(back, dest, rank)
    return within_max.reshape(-1), near_max.reshape(-1)


def solution(mesh):
    in_specs = (P(("shard", "blk"), None), P(("shard", "blk")), P(), P(), P())
    out_specs = (P(("shard", "blk")), P(("shard", "blk")))
    return jax.shard_map(
        on_device, mesh=mesh, in_specs=in_specs, out_specs=out_specs, check_vma=False
    )
```

```python
import functools

import jax
import jax.numpy as jnp
from jax import lax
from jax.experimental import pallas as pl
from jax.experimental.pallas import tpu as pltpu
from jax.sharding import PartitionSpec as P

EMB = 1024
SUBQ = 128
SUB = 8
CODES_K = 256
CPD = 8
LANES = 128
SHARDS = 16
CAP = 128
RECV = SHARDS * CAP
BLOCK = SUBQ + 16
norm_epsilon = 1e-06

VMEM = pl.BlockSpec(memory_space=pltpu.VMEM)


def lane_gather(table, index):
    numbers = lax.GatherDimensionNumbers(
        offset_dims=(),
        collapsed_slice_dims=(1,),
        start_index_map=(1,),
        operand_batching_dims=(0,),
        start_indices_batching_dims=(0,),
    )
    return lax.gather(
        table,
        index[..., None],
        numbers,
        slice_sizes=(1, 1),
        mode=lax.GatherScatterMode.PROMISE_IN_BOUNDS,
    )


def iota(shape, axis):
    return lax.broadcasted_iota(jnp.int32, shape, axis)


def route_kernel(
    codes_hbm, ids_hbm, owner_hbm, pair_hbm, send_hbm, dest_ref, rank_ref,
    codes_ref, ids_ref, owner_ref, pair_ref, send_ref, in_sem, out_sem,
):
    loads = [
        pltpu.make_async_copy(src, dst, in_sem.at[k])
        for k, (src, dst) in enumerate(
            [
                (owner_hbm, owner_ref),
                (ids_hbm, ids_ref),
                (pair_hbm, pair_ref),
                (codes_hbm, codes_ref),
            ]
        )
    ]
    for load in loads:
        load.start()
    column = lax.axis_index("blk")
    full = (8, LANES)
    sub, lane = iota((LANES, LANES), 0), iota((LANES, LANES), 1)
    loads[0].wait()
    loads[1].wait()
    owner_row = owner_ref[pl.ds(column, 1), :]
    local = ids_ref[...] - column * LANES
    dest = lane_gather(jnp.broadcast_to(owner_row, full), local)
    member = jnp.concatenate([(dest == o).astype(jnp.float32) for o in range(SHARDS)], axis=0)
    member = member.astype(jnp.bfloat16)
    before = (sub < lane).astype(jnp.bfloat16)
    in_row = jnp.dot(member, before, preferred_element_type=jnp.float32)
    above = ((sub // 8 == lane // 8) & (lane < sub)).astype(jnp.bfloat16)
    rows_above = jnp.dot(above, member, preferred_element_type=jnp.float32)
    count = in_row + jnp.sum(rows_above, axis=1, keepdims=True)
    rank = jnp.zeros(full, jnp.float32)
    for o in range(SHARDS):
        rank = jnp.where(dest == o, count[o * 8 : (o + 1) * 8, :], rank)
    rank = rank.astype(jnp.int32)
    dest_ref[...] = dest
    rank_ref[...] = rank
    owner_sq = jnp.broadcast_to(owner_row, (LANES, LANES))
    same = (owner_sq.T == owner_sq) & (sub < lane)
    slot_row = jnp.sum(same.astype(jnp.int32), axis=0, keepdims=True)
    slot = lane_gather(jnp.broadcast_to(slot_row, full), local)
    loads[2].wait()
    pair_row = pair_ref[pl.ds(column, 1), :]
    pair = lane_gather(jnp.broadcast_to(pair_row, full), local)
    slot_f = (slot + 1).astype(jnp.float32)
    pair_f = (pair + 1).astype(jnp.float32)
    slot_line = jnp.concatenate([slot_f[k : k + 1, :] for k in range(8)], axis=1)
    pair_line = jnp.concatenate([pair_f[k : k + 1, :] for k in range(8)], axis=1)
    tail_row = iota((16, 1024), 0)
    tail = jnp.where(tail_row == 0, slot_line, jnp.where(tail_row == 1, pair_line, 0.0))
    loads[3].wait()
    codes_t = codes_ref[...].astype(jnp.float32).T
    left = jnp.concatenate([codes_t, tail], axis=0).astype(jnp.bfloat16)
    stores = []
    for o in range(0, SHARDS, OWNERS):
        picks = []
        for p in range(OWNERS):
            key = jnp.where(dest == o + p, rank, -1)
            pick = [
                (jnp.broadcast_to(key[k : k + 1, :], (LANES, LANES)) == sub).astype(jnp.float32)
                for k in range(8)
            ]
            picks.append(jnp.concatenate(pick, axis=1))
        pick = jnp.concatenate(picks, axis=0).astype(jnp.bfloat16)
        block = lax.dot_general(
            left, pick, (((1,), (1,)), ((), ())), preferred_element_type=jnp.float32
        ).astype(jnp.bfloat16)
        for p in range(OWNERS):
            send_ref[o + p] = block[:, p * LANES : (p + 1) * LANES]
        part = pl.ds(o, OWNERS)
        store = pltpu.make_async_copy(
            send_ref.at[part], send_hbm.at[part], out_sem.at[o // OWNERS]
        )
        store.start()
        stores.append(store)
    for store in stores:
        store.wait()


OWNERS = 2


FOLD = 6
EARLY = 4
SIDE = 256
PER = SIDE // CAP
CHUNKS = RECV // SIDE
GROUP = 16
GROUPS = SUBQ // GROUP


def group_rows(g):
    if isinstance(g, int):
        return slice(g * GROUP, (g + 1) * GROUP)
    return pl.ds(pl.multiple_of(g * GROUP, GROUP), GROUP)


def codes_of(got_ref, block, g):
    return got_ref[block, group_rows(g), :].astype(jnp.int32)


def add_norms(got_ref, norm_ref, block, g, total):
    part = group_rows(g)
    code = codes_of(got_ref, block, g)
    rest = code & 127
    low, high = norm_ref[part, :LANES], norm_ref[part, LANES:]
    return total + jnp.where(code < LANES, lane_gather(low, rest), lane_gather(high, rest))


def scale_of(total):
    norm = jnp.sum(total, axis=0, keepdims=True)
    return jnp.broadcast_to(lax.rsqrt(norm + norm_epsilon), (GROUP, LANES))


def decode_part(got_ref, table_ref, block, g, scale, ut_ref, lanes):
    code = codes_of(got_ref, block, g).astype(jnp.int16)
    rest = code & 127
    is_low = code < LANES
    for i in range(SUB):
        low, high = table_ref[g, i, :, :LANES], table_ref[g, i, :, LANES:]
        value = jnp.where(is_low, lane_gather(low, rest), lane_gather(high, rest))
        rows = group_rows(g * SUB + i)
        ut_ref[rows, lanes] = (value.astype(jnp.float32) * scale).astype(jnp.bfloat16)


def block_lanes(j):
    return slice(j * LANES, (j + 1) * LANES)


def key_row(got_ref, j, line):
    return got_ref[j, SUBQ : SUBQ + 16, :].astype(jnp.float32)[line : line + 1, :]


def spread_keys(got_ref, line, keys_ref):
    for j in range(SHARDS):
        key = key_row(got_ref, j, line)
        keys_ref[j * LANES : (j + 1) * LANES, :] = jnp.broadcast_to(key, (LANES, LANES)).T


def key_line(got_ref, j, line):
    key = key_row(got_ref, j, line)
    return jnp.broadcast_to(jnp.where(key == 0.0, -1.0, key), (8, LANES))


def tiles(x):
    return x.reshape(x.shape[0] // 8, 8, LANES)


def fold_lanes(row_best):
    return jnp.max(row_best.T, axis=0, keepdims=True)


def parts_of(rows):
    half = RECV // 2
    return [slice(r, min(r + half, rows)) for r in range(0, rows, half)]


def scales(got_ref, norm_ref, n):
    totals = [jnp.zeros((GROUP, LANES), jnp.float32)] * PER
    for g in range(GROUPS):
        totals = [add_norms(got_ref, norm_ref, n * PER + h, g, totals[h]) for h in range(PER)]
    return [scale_of(t) for t in totals]


def chunk_scores(n, parts, u_ref, ut, keys_ref, line_of, best_ref, old_ref, own, between):
    cols = [jnp.full((8, LANES), -1.0, jnp.float32)] * PER
    for q, rows in enumerate(parts):
        scores = jnp.dot(u_ref[rows, :], ut[...], preferred_element_type=jnp.float32)
        between(q)
        key = tiles(keys_ref[rows, :])
        best = None if old_ref is None else tiles(old_ref[rows, :])
        for h in range(PER):
            part = tiles(scores[:, h * LANES : (h + 1) * LANES])
            ok = key == line_of(h)[None]
            if own and rows.stop > n * SIDE:
                row = iota(part.shape, 0) * 8 + iota(part.shape, 1)
                ok = ok & (row != iota(part.shape, 2) + (h * LANES + n * SIDE - rows.start))
            part = jnp.where(ok, part, -1.0)
            best = part if best is None else jnp.maximum(best, part)
            cols[h] = jnp.maximum(cols[h], jnp.max(part, axis=0))
        best_ref[rows, :] = best.reshape(rows.stop - rows.start, LANES)
    return [jnp.max(c, axis=0, keepdims=True) for c in cols]


def own_piece(n, got_ref, u_ref, ut_ref, keys_ref, best_ref, out_ref, between, alone=False):
    cols = chunk_scores(
        n,
        parts_of((n + 1) * SIDE),
        u_ref,
        ut_ref.at[:, n * SIDE : (n + 1) * SIDE],
        keys_ref,
        lambda h: key_line(got_ref, n * PER + h, 0),
        best_ref,
        None if alone else best_ref,
        True,
        between,
    )
    for h in range(PER):
        j = h if alone else n * PER + h
        out_ref[j : j + 1, :] = cols[h]


def own_kernel(
    got_ref, table_ref, norm_ref, ut_ref, u_ref, slots_ref, pairs_ref, best_ref, out_ref
):
    eye = (iota((SIDE, SIDE), 0) == iota((SIDE, SIDE), 1)).astype(jnp.bfloat16)

    def decode_chunk(n, groups, scale):
        for g in groups:
            for h in range(PER):
                j = n * PER + h
                decode_part(got_ref, table_ref, j, g, scale[h], ut_ref, block_lanes(j))

    def turn_chunk(n):
        lanes = slice(n * SIDE, (n + 1) * SIDE)
        u_ref[lanes, :] = lax.dot_general(
            eye, ut_ref[:, lanes], (((1,), (1,)), ((), ())), preferred_element_type=jnp.float32
        ).astype(jnp.bfloat16)

    spread_keys(got_ref, 0, slots_ref)
    spread_keys(got_ref, 1, pairs_ref)
    best_ref[...] = jnp.full(best_ref.shape, -1.0, jnp.float32)
    out_ref[...] = jnp.full(out_ref.shape, -1.0, jnp.float32)
    decode_chunk(0, range(GROUPS), scales(got_ref, norm_ref, 0))
    turn_chunk(0)
    for n in range(1, CHUNKS + 1):
        if n < CHUNKS:
            scale = scales(got_ref, norm_ref, n)
            if n - 1 >= EARLY:
                decode_chunk(n, range(GROUPS), scale)
        if n - 1 < EARLY:
            count = len(parts_of(n * SIDE))

            def between(q):
                if n < CHUNKS:
                    decode_chunk(n, range(q * GROUPS // count, (q + 1) * GROUPS // count), scale)

            own_piece(n - 1, got_ref, u_ref, ut_ref, slots_ref, best_ref, out_ref, between)
        if n < CHUNKS:
            turn_chunk(n)


def fold_rows(best_ref, out_ref, rows, join):
    for j in range(rows.start // LANES, rows.stop // LANES):
        row = fold_lanes(best_ref[j * LANES : (j + 1) * LANES, :])
        if join:
            row = jnp.maximum(out_ref[j : j + 1, :], row)
        out_ref[j : j + 1, :] = row


def within_kernel(
    got_ref, ut_ref, u_ref, slots_ref, best_in, early_in, best_more, more_in, crossed_ref,
    out_ref, row_ref, best_ref,
):
    out_ref[...] = early_in[...]
    out_ref[EARLY * PER : (EARLY + 1) * PER, :] = more_in[...]
    rows = (EARLY + 1) * SIDE
    best_ref[:rows, :] = jnp.maximum(best_in[:rows, :], best_more[...])
    best_ref[rows:, :] = best_in[rows:, :]
    parts = parts_of(RECV)

    def between(n, q):
        if n == FOLD:
            fold_rows(crossed_ref, row_ref, parts[q], False)
        if n == CHUNKS - 1 and q > 0:
            fold_rows(best_ref, out_ref, parts[q - 1], True)

    for n in range(EARLY + 1, CHUNKS):
        own_piece(
            n, got_ref, u_ref, ut_ref, slots_ref, best_ref, out_ref, lambda q: between(n, q)
        )
    fold_rows(best_ref, out_ref, parts[-1], True)


def decode_left(left_ref, table_ref, j, groups, scale, ut):
    for g in groups:
        for h in range(PER):
            decode_part(left_ref, table_ref, j + h, g, scale[h], ut, block_lanes(h))


def share(groups, q, count):
    return range(q * groups // count, (q + 1) * groups // count)


def left_scores(left_ref, j, pairs_ref, u_ref, ut, best_ref, old_ref, out_ref, row, between):
    cols = chunk_scores(
        0,
        parts_of(RECV),
        u_ref,
        ut,
        pairs_ref,
        lambda h: key_line(left_ref, j + h, 0),
        best_ref,
        old_ref,
        False,
        between,
    )
    for h in range(PER):
        out_ref[row + h : row + h + 1, :] = cols[h]


def first_kernel(
    pairs_ref, left_ref, table_ref, norm_ref, u_ref, got_ref, own_ref, slots_ref,
    out_ref, best_ref, ut_b, best_more, more_ref, ut_a,
):
    uts = (ut_a, ut_b)
    scale = scales(left_ref, norm_ref, 0)
    count = len(parts_of((EARLY + 1) * SIDE))
    own_piece(
        EARLY,
        got_ref,
        u_ref,
        own_ref,
        slots_ref,
        best_more,
        more_ref,
        lambda q: decode_left(left_ref, table_ref, 0, share(GROUPS, q, count), scale, ut_a),
        True,
    )
    for n in range(HALF // PER - 1):
        j = (n + 1) * PER
        scale = scales(left_ref, norm_ref, n + 1)
        left_scores(
            left_ref,
            n * PER,
            pairs_ref,
            u_ref,
            uts[n % 2],
            best_ref,
            best_ref if n else None,
            out_ref,
            n * PER,
            lambda q: decode_left(
                left_ref, table_ref, j, share(GROUPS, q, 2), scale, uts[(n + 1) % 2]
            ),
        )


def second_kernel(
    pairs_ref, before_ref, left_ref, table_ref, norm_ref, u_ref, best_in, ut_in,
    out_ref, best_ref, ut_a, ut_b,
):
    uts = (ut_in, ut_a, ut_b)
    chunks = HALF // PER
    for n in range(chunks + 1):
        now = uts[0] if n == 0 else uts[1 + (n - 1) % 2]
        scale = scales(left_ref, norm_ref, n) if n < chunks else None

        def between(q):
            if n < chunks:
                decode_left(
                    left_ref, table_ref, n * PER, share(GROUPS, q, 2), scale, uts[1 + n % 2]
                )

        left_scores(
            left_ref if n else before_ref,
            (n - 1) * PER if n else HALF - PER,
            pairs_ref,
            u_ref,
            now,
            best_ref,
            best_ref if n else best_in,
            out_ref,
            n * PER,
            between,
        )


def pick_kernel(got_ref, dest_ref, rank_ref, within_ref, near_ref):
    dest, rank = dest_ref[...], rank_ref[...]
    within = jnp.zeros((8, LANES), jnp.float32)
    near = within
    for o in range(SHARDS):
        here = dest == o
        first = jnp.broadcast_to(got_ref[o, 0:1, :], (8, LANES))
        second = jnp.broadcast_to(got_ref[o, 1:2, :], (8, LANES))
        within = jnp.where(here, lane_gather(first, rank), within)
        near = jnp.where(here, lane_gather(second, rank), near)
    within_ref[...] = within
    near_ref[...] = near


def kernel_call(body, shapes, count, scratch=(), name=None, flops=0):
    return pl.pallas_call(
        body,
        out_shape=shapes,
        in_specs=[VMEM] * count,
        out_specs=[VMEM] * len(shapes),
        scratch_shapes=list(scratch),
        compiler_params=pltpu.CompilerParams(vmem_limit_bytes=16 << 20),
        name=name,
        cost_estimate=pl.CostEstimate(flops=flops, bytes_accessed=1 << 20, transcendentals=0),
    )


def shape(dims, kind):
    return jax.ShapeDtypeStruct(dims, kind)


bf16, f32, i32 = jnp.bfloat16, jnp.float32, jnp.int32
K_OWN = (
    own_kernel,
    [
        shape((EMB, RECV), bf16),
        shape((RECV, EMB), bf16),
        shape((RECV, LANES), f32),
        shape((RECV, LANES), f32),
        shape((RECV, LANES), f32),
        shape((SHARDS, LANES), f32),
    ],
    3,
)
UT = pltpu.VMEM((EMB, SIDE), bf16)
BEST = pltpu.VMEM((RECV, LANES), f32)
HALF = SHARDS // 2
K_FIRST = (
    first_kernel,
    [
        shape((HALF - PER, LANES), f32),
        shape((RECV, LANES), f32),
        shape((EMB, SIDE), bf16),
        shape(((EARLY + 1) * SIDE, LANES), f32),
        shape((PER, LANES), f32),
    ],
    8,
    [UT],
)
K_SECOND = (
    second_kernel,
    [shape((HALF + PER, LANES), f32), shape((RECV, LANES), f32)],
    8,
    [UT, UT],
)
K_WITHIN = (
    within_kernel, [shape((SHARDS, LANES), f32), shape((SHARDS, LANES), f32)], 9, [BEST]
)
K_PICK = (pick_kernel, [shape((8, LANES), f32), shape((8, LANES), f32)], 3)


def route_call(*operands):
    small = pltpu.VMEM((8, LANES), i32)
    outside = pl.BlockSpec(memory_space=pltpu.HBM)
    return pl.pallas_call(
        route_kernel,
        out_shape=[
            shape((SHARDS, BLOCK, LANES), bf16),
            shape((8, LANES), i32),
            shape((8, LANES), i32),
        ],
        in_specs=[outside] * 4,
        out_specs=[outside, VMEM, VMEM],
        scratch_shapes=[
            pltpu.VMEM((SHARDS * 64, LANES), i32),
            small,
            small,
            small,
            pltpu.VMEM((SHARDS, BLOCK, LANES), bf16),
            pltpu.SemaphoreType.DMA((4,)),
            pltpu.SemaphoreType.DMA((SHARDS // OWNERS,)),
        ],
        compiler_params=pltpu.CompilerParams(vmem_limit_bytes=16 << 20),
        name="route",
    )(*[pltpu.with_memory_space_constraint(x, pltpu.HBM) for x in operands])


def from_behind(x, axis, by):
    peers = lax.axis_size(axis)
    return lax.ppermute(x, axis, [(i, (i + by) % peers) for i in range(peers)])


def tables_of(codebook):
    turned = jnp.swapaxes(codebook, 1, 2)
    wide = turned.astype(f32)
    norms = jnp.sum(wide * wide, axis=1)
    return turned.reshape(GROUPS, GROUP, SUB, CODES_K).transpose(0, 2, 1, 3), norms


def scores_of(got, left, table, norms):
    ut, u, slots, pairs, best, early = kernel_call(*K_OWN, name="own", flops=1 << 30)(
        got, table, norms
    )
    cols_a, partial, ut_last, best_more, more = kernel_call(
        *K_FIRST, name="first", flops=8 << 30
    )(pairs, left[0], table, norms, u, got, ut, slots)
    cols_b, crossed = kernel_call(*K_SECOND, name="second", flops=8 << 30)(
        pairs, left[0], left[1], table, norms, u, partial, ut_last
    )

    def within():
        return kernel_call(*K_WITHIN, name="within", flops=4 << 30)(
            got, ut, u, slots, best, early, best_more, more, crossed
        )

    return within, jnp.concatenate([cols_a, cols_b], axis=0)


def on_device(codes, cluster_ids, cluster_owner, left_pair, codebook):
    send, dest, rank = route_call(
        codes,
        cluster_ids.reshape(8, LANES),
        cluster_owner.reshape(8, LANES),
        left_pair.reshape(8, LANES),
    )
    table, norms = tables_of(codebook)
    got = lax.all_to_all(send, "shard", split_axis=0, concat_axis=0, tiled=True)
    got, table, norms = lax.optimization_barrier((got, table, norms))
    left = [from_behind(got[h * HALF : (h + 1) * HALF], "blk", 1) for h in range(2)]
    within, for_left = scores_of(got, left, table, norms)
    from_right = from_behind(for_left, "blk", -1)
    within, from_left = within()
    near = jnp.maximum(from_left, from_right)
    answers = jnp.stack([within, near], axis=1)
    back = lax.all_to_all(answers, "shard", split_axis=0, concat_axis=0, tiled=True)
    within_max, near_max = kernel_call(*K_PICK, name="pick")(back, dest, rank)
    return within_max.reshape(-1), near_max.reshape(-1)


def solution(mesh):
    in_specs = (P(("shard", "blk"), None), P(("shard", "blk")), P(), P(), P())
    out_specs = (P(("shard", "blk")), P(("shard", "blk")))
    return jax.shard_map(
        on_device, mesh=mesh, in_specs=in_specs, out_specs=out_specs, check_vma=False
    )
```
